32 devices in a mesh: sky: 4 (over y, x), freq: 8 (over z, core).
Axes of the slice: x: 2, y: 2, z: 4, core: 2. Of those that a mesh axis runs over, the one named last changes fastest.
Arguments:
- pieces: bfloat16 [32, 64, 128, 128], P('sky', 'freq'), may hold values from -120 to 120
- beam: bfloat16 [32, 128, 128], P('sky'), may hold values from 0.099609375 to 1
- destination: int32 [32], P('sky'), may hold values from 0 to 15, as said below
- clip_tenths: int32 [3, 4], replicated, may hold values from 30 to 60
Outputs:
- significance: float32 [64, 512, 512], P('freq', 'sky')
The draws below stay inside these ranges and needn't reach their ends.
Inputs may be any that keep to these rules, and one draw needn't show every extreme that they name: Among the 8 pieces of one index of sky, at most 4 have destinations in one tile, that is with equal destination // 4. In every draw some tile receives exactly 4 pieces from every index of sky.
All inputs are finite; a program needn't handle non-finite values.
Results may differ from the reference program's by a relative error of at most 0.0036.
Values may be sent and summed in bfloat16 or wider, within the bound.
No kernel may reach another device: no remote copies, remote signals or barrier semaphores. Data moves between devices by JAX's collectives and lax.ppermute only.
A program may use at most 128 MiB of HBM per device.

```python
import functools
import math
import jax
import jax.numpy as jnp
from jax import lax

BLK = 128
ROWB = 1
COLB = 4
RIM = 8
EDGE = 7
KERNELS = 3
WIDTHS = 4
PC_DEV = 8
CAP = 4
PIECES = 32
CH = 64
NY = 512
NX = 512
BLOCKS = 16
N_SKY = 4


def routing(key):
    owners = PIECES // PC_DEV
    tile_blocks = ROWB * COLB
    busiest = jax.random.randint(jax.random.fold_in(key, 101), (), 0, owners)

    def source(source_index):
        source_key = jax.random.fold_in(jax.random.fold_in(key, 202), source_index)
        spread = jax.random.permutation(jax.random.fold_in(source_key, 1), (owners - 1) * CAP)[:PC_DEV - CAP] // CAP
        spread = spread.astype(jnp.int32)
        spread = spread + (spread >= busiest).astype(jnp.int32)
        chosen = jnp.concatenate([jnp.full((CAP,), busiest, jnp.int32), spread])
        shuffle = jax.random.permutation(jax.random.fold_in(source_key, 2), PC_DEV)
        chosen = chosen[shuffle]
        within = jax.random.randint(jax.random.fold_in(source_key, 3), (PC_DEV,), 0, tile_blocks)
        return chosen * tile_blocks + within
    return jax.vmap(source)(jnp.arange(owners)).reshape(PIECES).astype(jnp.int32)


def draw_destination(key, part):
    return routing(key)


def spread_groups(grouped):
    return jnp.repeat(grouped, 8, axis=1)[:, :CH]


def draw_pieces(key, part):
    targets = routing(key)
    owners = PIECES // PC_DEV
    owner_tile = (targets // (ROWB * COLB)).astype(jnp.float32)
    position = owner_tile / float(max(owners - 1, 1))
    groups = (CH + 7) // 8
    group_shape = (PIECES, groups, BLK, BLK)
    shape = (PIECES, CH, BLK, BLK)
    shared_key = jax.random.fold_in(key, 404)
    own_key = jax.random.fold_in(key, 405)
    brightness = 1.0 + 2.0 * position
    limit = 4.0
    background = 0.012
    lowest = 1.8
    highest = 3.0
    shared = jnp.clip(jax.random.normal(shared_key, group_shape, jnp.float32), -4.0, 4.0)
    own = jnp.clip(jax.random.normal(own_key, shape, jnp.float32), -4.0, 4.0)
    present = jax.random.bernoulli(jax.random.fold_in(key, 406), 1.0 / 32768.0, group_shape).astype(jnp.float32)
    signs = jnp.where(jax.random.bernoulli(jax.random.fold_in(key, 407), 0.5, group_shape), 1.0, -1.0)
    amplitude = jax.random.uniform(jax.random.fold_in(key, 408), group_shape, jnp.float32, lowest, highest) * signs * present
    cluster = amplitude + 0.6 * jnp.roll(amplitude, 1, axis=3) + 0.4 * jnp.roll(amplitude, 1, axis=2)
    base = spread_groups(cluster) + background * (0.9 * spread_groups(shared) + 0.45 * own)
    base = jnp.clip(base, -limit, limit)
    channel_scale = jnp.exp(jax.random.uniform(jax.random.fold_in(key, 303), (CH,), jnp.float32, 0.0, math.log(10.0)))
    return (base * brightness[:, None, None, None] * channel_scale[None, :, None, None]).astype(jnp.bfloat16)


def place_ends(entries, stream_key, least, top_value):
    longest = entries.shape.index(max(entries.shape))
    spots = []
    for shift in (0, 1):
        where = [jax.random.randint(jax.random.fold_in(stream_key, axis), (), 0, length) for axis, length in enumerate(entries.shape)]
        where[longest] = (where[longest] + shift) % entries.shape[longest]
        spots.append(tuple(where))
    return entries.at[spots[0]].set(least).at[spots[1]].set(top_value)


def levels(stream_key, extent, shards, smallest, high):
    factor_of = 1.0
    for dim, blocks in shards:
        draws = jax.random.uniform(jax.random.fold_in(jax.random.fold_in(stream_key, 6), dim), (blocks,), jnp.float32, smallest / len(shards), high / len(shards))
        factor_of = factor_of * jnp.repeat(jnp.exp(draws), extent[dim] // blocks).reshape((-1,) + (1,) * (len(extent) - 1 - dim))
    return factor_of


def setup_inputs(seed: int = 0) -> dict:
    seeds = jax.random.split(jax.random.key(seed), 5)
    pieces = draw_pieces(jax.random.fold_in(seeds[4], 71), 0)
    beam = jnp.clip(jnp.exp(math.log(1.0) - 2.306499 * jax.random.uniform(seeds[1], (PIECES, BLK, BLK), jnp.float32) ** levels(seeds[1], (PIECES, BLK, BLK), ((0, 4),), -0.2, 0.2)), 0.099609375, 1.0).astype(jnp.bfloat16)
    destination = draw_destination(jax.random.fold_in(seeds[4], 71), 0)
    clip_tenths = place_ends(jax.random.randint(seeds[3], (KERNELS, WIDTHS), 30, 61), jax.random.fold_in(seeds[3], 1), 30, 60).astype(jnp.int32)
    return dict(pieces=pieces, beam=beam, destination=destination, clip_tenths=clip_tenths)


REGULARIZER = 0.05
EPSILON = 1e-06
KERNEL_FWHM = (3.0, 6.0, 9.0)
HALF_WIDTHS = (0, 1, 3, 7)

def kernel_taps(kernel):
    offsets = jnp.arange(-RIM, RIM + 1).astype(jnp.float32)
    sigma = KERNEL_FWHM[kernel] / 2.3548
    values = jnp.exp(-offsets * offsets / (2.0 * sigma * sigma))
    return lax.optimization_barrier(values.astype(jnp.bfloat16)).astype(jnp.float32)

def smooth_plane(weights, channel_plane):
    widened = jnp.pad(channel_plane.astype(jnp.float32), ((0, 0), (RIM, RIM)))
    across = jnp.zeros((NY, NX), jnp.float32)
    for offset in range(2 * RIM + 1):
        across = across + weights[offset] * widened[:, offset:offset + NX]
    across = lax.optimization_barrier(across.astype(jnp.bfloat16)).astype(jnp.float32)
    taller = jnp.pad(across, ((RIM, RIM), (0, 0)))
    result = jnp.zeros((NY, NX), jnp.float32)
    for offset in range(2 * RIM + 1):
        result = result + weights[offset] * taller[offset:offset + NY, :]
    return result.astype(jnp.bfloat16)

def boxcars(layer, channel):
    window = lax.dynamic_slice_in_dim(layer, channel, 2 * EDGE + 1, 0).astype(jnp.float32)
    running = window[EDGE]
    found = [running]
    for step in range(1, EDGE + 1):
        running = running + window[EDGE - step] + window[EDGE + step]
        if step in HALF_WIDTHS:
            found.append(running)
    return found

def reference(pieces, beam, destination, clip_tenths):
    beam_wide = beam.astype(jnp.float32)
    coverage = jax.ops.segment_sum(beam_wide * beam_wide, destination, num_segments=BLOCKS) + REGULARIZER

    def combined_plane(channel_pieces):
        weighted = lax.optimization_barrier((beam_wide * channel_pieces.astype(jnp.float32)).astype(jnp.bfloat16)).astype(jnp.float32)
        numerator = jax.ops.segment_sum(weighted, destination, num_segments=BLOCKS)
        blocks = (numerator / coverage).astype(jnp.bfloat16)
        arranged = blocks.reshape(N_SKY, ROWB, COLB, BLK, BLK).transpose(0, 1, 3, 2, 4)
        return arranged.reshape(NY, NX)
    combined = lax.map(combined_plane, jnp.moveaxis(pieces, 1, 0))
    padded = []
    for kernel in range(KERNELS):
        weights = kernel_taps(kernel)
        smoothed = lax.map(functools.partial(smooth_plane, weights), combined)
        padded.append(jnp.pad(smoothed, ((EDGE, EDGE), (0, 0), (0, 0))))

    def channel_power(channel):
        rows_out = []
        for layer in padded:
            rows_out.append(jnp.stack([jnp.sum(found * found) for found in boxcars(layer, channel)]))
        return jnp.stack(rows_out)
    channels = jnp.arange(CH).astype(jnp.int32)
    powers = lax.map(channel_power, channels)
    noise_level = jnp.sqrt(powers / float(NY * NX) + EPSILON)
    factor = 10.0 / (clip_tenths.astype(jnp.float32)[None] * noise_level)

    def channel_score(inputs):
        channel, scales = inputs
        best = jnp.zeros((NY, NX), jnp.float32)
        for kernel in range(KERNELS):
            for width, running in enumerate(boxcars(padded[kernel], channel)):
                best = jnp.maximum(best, jnp.abs(running) * scales[kernel, width])
        return best
    return lax.map(channel_score, (channels, factor))
```

```python
import functools

import jax
import jax.numpy as jnp
import ml_dtypes
import numpy as np
from jax import lax
from jax.experimental import pallas as pl
from jax.experimental.pallas import tpu as pltpu
from jax.sharding import PartitionSpec as P

ROWB = 1
COLB = 4
RIM = 8
EDGE = 7
KERNELS = 3
WIDTHS = 4

REGULARIZER = 0.05
EPSILON = 1e-06
KERNEL_FWHM = (3.0, 6.0, 9.0)
HALF_WIDTHS = (0, 1, 3, 7)

LANES = 128
MIB = 1 << 20
F32 = jnp.float32
BF16 = jnp.bfloat16
SMEM = pl.BlockSpec(memory_space=pltpu.SMEM)
VMEM = pl.BlockSpec(memory_space=pltpu.VMEM)


def params(mib):
    return pltpu.CompilerParams(vmem_limit_bytes=mib * MIB)


def cost(flops, moved):
    return pl.CostEstimate(flops=int(flops), bytes_accessed=int(moved), transcendentals=0)


def tap_table(distance):
    offsets = np.arange(-RIM, RIM + 1).astype(np.float32)
    near = np.abs(distance) <= RIM
    index = np.clip(distance + RIM, 0, 2 * RIM)
    found = []
    for fwhm in KERNEL_FWHM:
        sigma = np.float32(fwhm / 2.3548)
        taps = np.exp(-offsets * offsets / (np.float32(2.0) * sigma * sigma)).astype(ml_dtypes.bfloat16)
        found.append(np.where(near, taps[index], np.zeros((), ml_dtypes.bfloat16)))
    return np.stack(found)


def across_matrices(broad):
    cells = np.arange(broad)
    return tap_table(cells[:, None] - cells[None, :])


def down_matrices(count, strip):
    tall = count * strip
    found = []
    for me in range(count):
        rows = [(me ^ k) * strip + np.arange(strip) for k in range(count)]
        rows += [np.arange(-RIM, 0), np.arange(tall, tall + RIM)]
        rows = np.concatenate(rows)
        found.append(tap_table(rows[None, :] - np.arange(tall)[:, None]).reshape(KERNELS * tall, tall + 2 * RIM))
    return np.stack(found)


def exchange(block, axis, k):
    count = lax.axis_size(axis)
    return lax.ppermute(block, axis, [(i, i ^ k) for i in range(count)])


def pack_kernel(me_ref, pieces_ref, beam_ref, *outs):
    channels = pieces_ref.shape[1]
    me = me_ref[0]
    for k, out in enumerate(outs):
        strip = me ^ k
        beam = beam_ref[:, strip]
        wide = beam.astype(F32)
        for c in range(channels):
            out[:, c] = (wide * pieces_ref[:, c, strip].astype(F32)).astype(BF16)
        out[:, channels] = beam


def pack(me, pieces, beam, count):
    piece_count, channels, size, _ = pieces.shape
    strip = size // count
    step = 2
    parts = pieces.reshape(piece_count, channels, count, strip, LANES)
    beams = beam.reshape(piece_count, count, strip, LANES)
    out = jax.ShapeDtypeStruct((piece_count, channels + 1, strip, LANES), BF16)
    return pl.pallas_call(
        pack_kernel,
        grid=(piece_count // step,),
        in_specs=[
            SMEM,
            pl.BlockSpec((step, channels, count, strip, LANES), lambda i: (i, 0, 0, 0, 0)),
            pl.BlockSpec((step, count, strip, LANES), lambda i: (i, 0, 0, 0)),
        ],
        out_specs=[pl.BlockSpec((step, channels + 1, strip, LANES), lambda i: (i, 0, 0, 0))] * count,
        out_shape=[out] * count,
        compiler_params=params(24),
        cost_estimate=cost(pieces.size, 4 * pieces.size),
        name="pack_pieces",
    )(me, parts, beams)


def combine_kernel(count, me_ref, owner_ref, *refs):
    parts, outs = refs[:count], refs[count : 2 * count]
    total, cover = refs[2 * count :]
    piece_count, planes, strip, _ = parts[0].shape
    channels = planes - 1
    me = me_ref[0]
    total[...] = jnp.zeros_like(total)
    cover[...] = jnp.full(cover.shape, REGULARIZER, F32)
    for k, part in enumerate(parts):
        source = me ^ k

        def add(p, _, part=part, source=source):
            block = owner_ref[source, p]
            beam = part[p, channels].astype(F32)
            cover[block] += beam * beam
            total[block] += part[p, :channels].astype(F32)
            return 0

        lax.fori_loop(0, piece_count, add, 0)
    first = me == 0
    last = me == count - 1
    for k, out in enumerate(outs):
        tile = me ^ k
        other = jnp.where(last, tile - 1, tile + 1)
        valid = jnp.logical_or(
            jnp.logical_and(last, tile > 0), jnp.logical_and(first, tile < count - 1)
        )
        other = jnp.clip(other, 0, count - 1)
        for column in range(COLB):
            lanes = slice(column * LANES, (column + 1) * LANES)
            block = tile * COLB + column
            scale = 1.0 / cover[block]
            for c in range(channels):
                out[c, :, lanes] = (total[block, c] * scale).astype(BF16)
            block = other * COLB + column
            rows = []
            for c in range(channels):
                high = total[block, c, strip - RIM :] / cover[block, strip - RIM :]
                low = total[block, c, :RIM] / cover[block, :RIM]
                rows.append(jnp.where(valid, jnp.where(last, high, low), 0.0))
            rims = jnp.concatenate(rows, axis=0)
            for e in range(channels * RIM // strip):
                out[channels + e, :, lanes] = rims[e * strip : (e + 1) * strip].astype(BF16)


def combine(me, owners, parts, count):
    piece_count, planes, strip, _ = parts[0].shape
    channels = planes - 1
    out = jax.ShapeDtypeStruct((channels + channels * RIM // strip, strip, COLB * LANES), BF16)
    blocks = count * COLB
    return pl.pallas_call(
        functools.partial(combine_kernel, count),
        in_specs=[SMEM, SMEM] + [VMEM] * count,
        out_specs=[VMEM] * count,
        out_shape=[out] * count,
        scratch_shapes=[
            pltpu.VMEM((blocks, channels, strip, LANES), F32),
            pltpu.VMEM((blocks, strip, LANES), F32),
        ],
        compiler_params=params(32),
        cost_estimate=cost(4 * count * parts[0].size, 4 * count * parts[0].size),
        name="combine_strips",
    )(me, owners, *parts)


def assemble_kernel(count, me_ref, *refs):
    parts, (full, lower, upper) = refs[:count], refs[count:]
    channels, tall, broad = full.shape
    strip = parts[0].shape[1]
    me = me_ref[0]

    def place(c, value, start):
        size = value.shape[0]
        full[c, start : start + size] = value
        if c < EDGE:
            lower[c, start : start + size] = value
        if c >= channels - EDGE:
            upper[c - (channels - EDGE), start : start + size] = value

    rims = [part[channels:].astype(F32).reshape(channels, RIM, broad) for part in parts]
    for c in range(channels):
        above = jnp.zeros((RIM, broad), F32)
        below = jnp.zeros((RIM, broad), F32)
        for k, rim in enumerate(rims):
            source = me ^ k
            above = jnp.where(source == count - 1, rim[c], above)
            below = jnp.where(source == 0, rim[c], below)
        edges = jnp.concatenate([above, below], axis=0).astype(BF16)
        if strip % 16 == 0:
            for k, part in enumerate(parts):
                place(c, part[c], k * strip)
        else:
            body = jnp.concatenate([part[c].astype(F32) for part in parts], axis=0)
            place(c, body.astype(BF16), 0)
        place(c, edges, count * strip)


def assemble(me, parts, channels, count):
    _, strip, broad = parts[0].shape
    tall = count * strip + 2 * RIM
    full = jax.ShapeDtypeStruct((channels, tall, broad), BF16)
    side = jax.ShapeDtypeStruct((EDGE, tall, broad), BF16)
    return pl.pallas_call(
        functools.partial(assemble_kernel, count),
        in_specs=[SMEM] + [VMEM] * count,
        out_specs=[VMEM] * 3,
        out_shape=[full, side, side],
        compiler_params=params(24),
        cost_estimate=cost(full.size, 8 * full.size),
        name="assemble_tile",
    )(me, *parts)


def smooth_planes(source, down, across, middle, write):
    planes, _, broad = source.shape
    tall = down.shape[0] // KERNELS

    def rows(c, _):
        found = jnp.dot(down[...], source[c], preferred_element_type=F32).astype(BF16)
        for k in range(KERNELS):
            middle[k, c] = found[k * tall : (k + 1) * tall]
        return 0

    def columns(c, _):
        for k in range(KERNELS):
            write(k, c, jnp.dot(middle[k, c], across[k], preferred_element_type=F32).astype(BF16))
        return 0

    lax.fori_loop(0, planes, rows, 0)
    lax.fori_loop(0, planes, columns, 0)


def smooth_kernel(source, down, across, out, middle):
    def write(k, c, value):
        out[k, c] = value

    smooth_planes(source, down, across, middle, write)


def smooth(source, down, across):
    planes, _, broad = source.shape
    tall = down.shape[0] // KERNELS
    out = jax.ShapeDtypeStruct((KERNELS, planes, tall, broad), BF16)
    return pl.pallas_call(
        smooth_kernel,
        in_specs=[VMEM] * 3,
        out_specs=VMEM,
        out_shape=out,
        scratch_shapes=[pltpu.VMEM((KERNELS, planes, tall, broad), BF16)],
        compiler_params=params(32),
        cost_estimate=cost(2 * out.size * (broad + 256), 4 * out.size),
        name="smooth_own",
    )(source, down, across)


def boxcars(layers):
    channels = len(layers) - 2 * EDGE

    @functools.cache
    def run(length, i):
        if length == 1:
            return layers[i]
        half = length // 2
        return run(half, i) + run(half, i + half)

    @functools.cache
    def box(half, i):
        if half == 0:
            return layers[i]
        return run(half + 1, i - half) + box(half // 2, i + (half + 1) // 2)

    return [[box(half, c + EDGE) for c in range(channels)] for half in HALF_WIDTHS]


def load_layers(own, halo, k, rows, lanes):
    channels = own.shape[1]
    refs = [(halo, c) for c in range(EDGE)]
    refs += [(own, c) for c in range(channels)]
    refs += [(halo, c) for c in range(EDGE, 2 * EDGE)]
    return [ref[k, c, rows, lanes].astype(F32).reshape(-1, 8, LANES) for ref, c in refs]


def power_kernel(low, high, own, down, across, halo, power, middle, sums):
    tall, broad = own.shape[2:]
    channels = own.shape[1]
    for side, start in ((low, 0), (high, EDGE)):

        def write(k, c, value, start=start):
            halo[k, start + c] = value

        smooth_planes(side, down, across, middle, write)
    sums[...] = jnp.zeros_like(sums)
    groups = broad // LANES

    def add(step, _):
        rows = pl.ds(pl.multiple_of(step // groups * 16, 16), 16)
        lanes = pl.ds(pl.multiple_of(step % groups * LANES, LANES), LANES)
        for k in range(KERNELS):
            found = boxcars(load_layers(own, halo, k, rows, lanes))
            for w in range(WIDTHS):
                for c in range(channels):
                    square = found[w][c] * found[w][c]
                    sums[(k * WIDTHS + w) * channels + c] += jnp.sum(square, axis=0)
        return 0

    lax.fori_loop(0, tall // 16 * groups, add, 0)
    total = jnp.sum(jnp.sum(sums[...], axis=1), axis=1, keepdims=True)
    power[...] = jnp.broadcast_to(total, power.shape)


def smooth_halo_power(low, high, own, down, across):
    _, channels, tall, broad = own.shape
    pairs = KERNELS * WIDTHS * channels
    halo = jax.ShapeDtypeStruct((KERNELS, 2 * EDGE, tall, broad), BF16)
    return pl.pallas_call(
        power_kernel,
        in_specs=[VMEM] * 5,
        out_specs=[VMEM] * 2,
        out_shape=[halo, jax.ShapeDtypeStruct((pairs, LANES), F32)],
        scratch_shapes=[
            pltpu.VMEM((KERNELS, EDGE, tall, broad), BF16),
            pltpu.VMEM((pairs, 8, LANES), F32),
        ],
        compiler_params=params(48),
        cost_estimate=cost(2 * halo.size * (broad + 256), 8 * halo.size),
        name="smooth_halo_power",
    )(low, high, own, down, across)


def score_kernel(count, cells, own, halo, clips, *refs):
    powers, (out, factor) = refs[:count], refs[count:]
    channels, tall, broad = out.shape

    @pl.when(pl.program_id(0) == 0)
    def _():
        total = powers[0][...]
        for item in powers[1:]:
            total = total + item[...]
        scale = 10.0 / (clips[...] * jnp.sqrt(total / cells + EPSILON))
        factor[...] = jnp.broadcast_to(scale[:, None], factor.shape)

    groups = broad // LANES

    def score(step, _):
        rows = pl.ds(pl.multiple_of(step // groups * 16, 16), 16)
        lanes = pl.ds(pl.multiple_of(step % groups * LANES, LANES), LANES)
        best = [None] * channels
        for k in range(KERNELS):
            found = boxcars(load_layers(own, halo, k, rows, lanes))
            for w in range(WIDTHS):
                for c in range(channels):
                    value = jnp.abs(found[w][c]) * factor[(k * WIDTHS + w) * channels + c]
                    best[c] = value if best[c] is None else jnp.maximum(best[c], value)
        for c in range(channels):
            out[c, rows, lanes] = best[c].reshape(16, LANES)
        return 0

    lax.fori_loop(0, tall // 16 * groups, score, 0)


def score(own, halo, clips, powers, cells):
    _, channels, tall, broad = own.shape
    pairs = KERNELS * WIDTHS * channels
    count = len(powers)
    step = 32
    return pl.pallas_call(
        functools.partial(score_kernel, count, cells),
        grid=(tall // step,),
        in_specs=[
            pl.BlockSpec((KERNELS, channels, step, broad), lambda i: (0, 0, i, 0)),
            pl.BlockSpec((KERNELS, 2 * EDGE, step, broad), lambda i: (0, 0, i, 0)),
        ]
        + [pl.BlockSpec((pairs, LANES), lambda i: (0, 0))] * (1 + count),
        out_specs=pl.BlockSpec((channels, step, broad), lambda i: (0, i, 0)),
        out_shape=jax.ShapeDtypeStruct((channels, tall, broad), F32),
        scratch_shapes=[pltpu.VMEM((pairs, 8, LANES), F32)],
        compiler_params=params(40),
        cost_estimate=cost(40 * KERNELS * own.size, 8 * own.size),
        name="score_cells",
    )(own, halo, clips, *powers)


def shards(across_table, down_table, pieces, beam, destination, clip_tenths):
    count = lax.axis_size("sky")
    links = lax.axis_size("freq")
    channels = pieces.shape[1]
    me = lax.axis_index("sky")
    place = me.astype(jnp.int32).reshape(1)
    owners = lax.all_gather(destination, "sky")
    packed = pack(place, pieces, beam, count)
    arrived = [packed[0]] + [exchange(packed[k], "sky", k) for k in range(1, count)]
    strips = combine(place, owners, arrived, count)
    tiles = [strips[0]] + [exchange(strips[k], "sky", k) for k in range(1, count)]
    full, lower, upper = assemble(place, tiles, channels, count)
    low = lax.ppermute(upper, "freq", [(i, i + 1) for i in range(links - 1)])
    high = lax.ppermute(lower, "freq", [(i + 1, i) for i in range(links - 1)])
    across = jnp.asarray(across_table)
    down = lax.dynamic_index_in_dim(jnp.asarray(down_table), me, 0, keepdims=False)
    own = smooth(full, down, across)
    halo, power = smooth_halo_power(low, high, own, down, across)
    powers = [power] + [exchange(power, "sky", k) for k in range(1, count)]
    clips = jnp.repeat(clip_tenths.astype(F32).reshape(-1), channels)
    clips = jnp.broadcast_to(clips[:, None], power.shape)
    cells = float(count * ROWB * LANES * COLB * LANES)
    return score(own, halo, clips, powers, cells)


def solution(mesh):
    count = mesh.shape["sky"]
    body = functools.partial(
        shards, across_matrices(COLB * LANES), down_matrices(count, ROWB * LANES // count)
    )
    return jax.shard_map(
        body,
        mesh=mesh,
        in_specs=(P("sky", "freq", None, None), P("sky", None, None), P("sky"), P()),
        out_specs=P("freq", "sky", None),
        check_vma=False,
    )
```

```python
import functools

import jax
import jax.numpy as jnp
import ml_dtypes
import numpy as np
from jax import lax
from jax.experimental import pallas as pl
from jax.experimental.pallas import tpu as pltpu
from jax.sharding import PartitionSpec as P

ROWB = 1
COLB = 4
RIM = 8
EDGE = 7
KERNELS = 3
WIDTHS = 4

REGULARIZER = 0.05
EPSILON = 1e-06
KERNEL_FWHM = (3.0, 6.0, 9.0)
HALF_WIDTHS = (0, 1, 3, 7)

LANES = 128
MIB = 1 << 20
F32 = jnp.float32
BF16 = jnp.bfloat16
SMEM = pl.BlockSpec(memory_space=pltpu.SMEM)
VMEM = pl.BlockSpec(memory_space=pltpu.VMEM)


def params(mib):
    return pltpu.CompilerParams(vmem_limit_bytes=mib * MIB)


def cost(flops, moved):
    return pl.CostEstimate(flops=int(flops), bytes_accessed=int(moved), transcendentals=0)


def tap_table(distance):
    offsets = np.arange(-RIM, RIM + 1).astype(np.float32)
    near = np.abs(distance) <= RIM
    index = np.clip(distance + RIM, 0, 2 * RIM)
    found = []
    for fwhm in KERNEL_FWHM:
        sigma = np.float32(fwhm / 2.3548)
        taps = np.exp(-offsets * offsets / (np.float32(2.0) * sigma * sigma)).astype(ml_dtypes.bfloat16)
        found.append(np.where(near, taps[index], np.zeros((), ml_dtypes.bfloat16)))
    return np.stack(found)


def across_matrices(broad):
    half = broad // 2
    cells = np.arange(broad)
    table = tap_table(cells[:, None] - cells[None, :])
    middle = slice(half // 2, half // 2 + half)
    seam = (cells[middle, None] < half) != (cells[None, middle] < half)
    crossing = np.where(seam[None], table[:, middle, middle], np.zeros((), ml_dtypes.bfloat16))
    return np.stack([table[:, :half, :half], table[:, half:, half:], crossing], axis=1)


def down_matrices(count, strip):
    tall = count * strip
    found = []
    for me in range(count):
        rows = [(me ^ k) * strip + np.arange(strip) for k in range(count)]
        rows += [np.arange(-RIM, 0), np.arange(tall, tall + RIM)]
        rows = np.concatenate(rows)
        found.append(tap_table(rows[None, :] - np.arange(tall)[:, None]).reshape(KERNELS * tall, tall + 2 * RIM))
    return np.stack(found)


def exchange(block, axis, k):
    count = lax.axis_size(axis)
    return lax.ppermute(block, axis, [(i, i ^ k) for i in range(count)])


def pack_kernel(count, groups, me_ref, owner_ref, pieces_ref, beam_ref, *outs):
    step, channels = pieces_ref.shape[:2]
    strip = pieces_ref.shape[3]
    me = me_ref[0]
    wide_group = channels // groups
    i = pl.program_id(0)

    for k in range(count):
        target = me ^ k
        for p in range(step):
            beam = beam_ref[p, target]
            wide = beam.astype(F32)
            piece = i * step + p
            for g in range(groups):
                out = outs[g * count + k]
                planes = wide_group + (g == 0)
                for c in range(wide_group):
                    value = wide * pieces_ref[p, g * wide_group + c, target].astype(F32)
                    out[piece * planes + c] = value.astype(BF16)
                if g == 0:
                    out[piece * planes + wide_group] = beam

    @pl.when(i == 0)
    def _():
        row = lax.broadcasted_iota(jnp.int32, (strip, LANES), 0)
        plane = jnp.zeros((strip, LANES), jnp.int32)
        for p in range(owner_ref.shape[0]):
            plane = jnp.where(row == p, owner_ref[p], plane)
        for k in range(count):
            out = outs[k]
            out[out.shape[0] - 1] = plane.astype(F32).astype(BF16)


def pack(me, destination, pieces, beam, count, groups):
    piece_count, channels, size, _ = pieces.shape
    strip = size // count
    step = 2
    parts = pieces.reshape(piece_count, channels, count, strip, LANES)
    beams = beam.reshape(piece_count, count, strip, LANES)
    planes = [piece_count * (channels // groups + (g == 0)) + (g == 0) for g in range(groups)]
    outs = [jax.ShapeDtypeStruct((planes[g], strip, LANES), BF16) for g in range(groups) for _ in range(count)]
    found = pl.pallas_call(
        functools.partial(pack_kernel, count, groups),
        grid=(piece_count // step,),
        in_specs=[
            SMEM,
            SMEM,
            pl.BlockSpec((step, channels, count, strip, LANES), lambda i: (i, 0, 0, 0, 0)),
            pl.BlockSpec((step, count, strip, LANES), lambda i: (i, 0, 0, 0)),
        ],
        out_specs=[pl.BlockSpec(out.shape, lambda i: (0, 0, 0)) for out in outs],
        out_shape=outs,
        compiler_params=params(56),
        cost_estimate=cost(pieces.size, 4 * pieces.size),
        name="pack_pieces",
    )(me, destination, parts, beams)
    return [found[g * count : (g + 1) * count] for g in range(groups)]


def write_strips(count, me, scale, total, outs):
    _, channels, strip, _ = total.shape
    first = me == 0
    last = me == count - 1
    for k, out in enumerate(outs):
        tile = me ^ k
        other = jnp.where(last, tile - 1, tile + 1)
        valid = jnp.logical_or(
            jnp.logical_and(last, tile > 0), jnp.logical_and(first, tile < count - 1)
        )
        other = jnp.clip(other, 0, count - 1)
        for column in range(COLB):
            lanes = slice(column * LANES, (column + 1) * LANES)
            block = tile * COLB + column
            factor = scale[block]
            for c in range(channels):
                out[c, :, lanes] = (total[block, c] * factor).astype(BF16)
            block = other * COLB + column
            rows = []
            for c in range(channels):
                high = total[block, c, strip - RIM :] * scale[block, strip - RIM :]
                low = total[block, c, :RIM] * scale[block, :RIM]
                rows.append(jnp.where(valid, jnp.where(last, high, low), 0.0))
            rims = jnp.concatenate(rows, axis=0)
            for e in range(channels * RIM // strip):
                out[channels + e, :, lanes] = rims[e * strip : (e + 1) * strip].astype(BF16)


def combine_first_kernel(count, piece_count, me_ref, *refs):
    parts, outs = refs[:count], refs[count : 2 * count]
    scale, owners, total, cover, rows, table, sem = refs[2 * count :]
    planes = (parts[0].shape[0] - 1) // piece_count
    channels = planes - 1
    me = me_ref[0]
    for k, part in enumerate(parts):
        plane = part[part.shape[0] - 1].astype(F32)[:piece_count]
        rows[k * piece_count : (k + 1) * piece_count] = plane.astype(jnp.int32)
    copy = pltpu.make_async_copy(rows, table, sem)
    copy.start()
    total[...] = jnp.zeros_like(total)
    cover[...] = jnp.full(cover.shape, REGULARIZER, F32)
    copy.wait()
    for k, part in enumerate(parts):

        def add(p, _, k=k, part=part):
            block = table[k * piece_count + p, 0]
            owners[k, p] = block
            beam = part[p * planes + channels].astype(F32)
            cover[block] += beam * beam
            total[block] += part[pl.ds(p * planes, channels)].astype(F32)
            return 0

        lax.fori_loop(0, piece_count, add, 0)
    scale[...] = 1.0 / cover[...]
    write_strips(count, me, scale, total, outs)


def combine_next_kernel(count, piece_count, me_ref, owners, scale, *refs):
    parts, outs, total = refs[:count], refs[count : 2 * count], refs[2 * count]
    channels = parts[0].shape[0] // piece_count
    total[...] = jnp.zeros_like(total)
    for k, part in enumerate(parts):

        def add(p, _, k=k, part=part):
            total[owners[k, p]] += part[pl.ds(p * channels, channels)].astype(F32)
            return 0

        lax.fori_loop(0, piece_count, add, 0)
    write_strips(count, me_ref[0], scale, total, outs)


def combine(me, known, parts, channels, piece_count, count):
    strip = parts[0].shape[1]
    out = jax.ShapeDtypeStruct((channels + channels * RIM // strip, strip, COLB * LANES), BF16)
    blocks = count * COLB
    total = pltpu.VMEM((blocks, channels, strip, LANES), F32)
    common = dict(
        compiler_params=params(24),
        cost_estimate=cost(4 * count * parts[0].size, 4 * count * parts[0].size),
    )
    if known is None:
        found = pl.pallas_call(
            functools.partial(combine_first_kernel, count, piece_count),
            in_specs=[SMEM] + [VMEM] * count,
            out_specs=[VMEM] * (count + 1) + [SMEM],
            out_shape=[out] * count
            + [
                jax.ShapeDtypeStruct((blocks, strip, LANES), F32),
                jax.ShapeDtypeStruct((count, piece_count), jnp.int32),
            ],
            scratch_shapes=[
                total,
                pltpu.VMEM((blocks, strip, LANES), F32),
                pltpu.VMEM((count * piece_count, LANES), jnp.int32),
                pltpu.SMEM((count * piece_count, LANES), jnp.int32),
                pltpu.SemaphoreType.DMA,
            ],
            name="combine_first",
            **common,
        )(me, *parts)
        return found[:count], found[count:]
    scale, owners = known
    found = pl.pallas_call(
        functools.partial(combine_next_kernel, count, piece_count),
        in_specs=[SMEM, SMEM, VMEM] + [VMEM] * count,
        out_specs=[VMEM] * count,
        out_shape=[out] * count,
        scratch_shapes=[total],
        name="combine_next",
        **common,
    )(me, owners, scale, *parts)
    return found, known


def assemble_kernel(count, ranges, me_ref, *refs):
    parts, outs = refs[:count], refs[count:]
    channels, tall, broad = outs[0].shape
    strip = parts[0].shape[1]
    me = me_ref[0]

    def place(c, value, start):
        size = value.shape[0]
        for out, (low, high) in zip(outs, ranges):
            if low <= c < high:
                out[c - low, start : start + size] = value

    rims = [part[channels:].astype(F32).reshape(channels, RIM, broad) for part in parts]
    for c in range(channels):
        above = jnp.zeros((RIM, broad), F32)
        below = jnp.zeros((RIM, broad), F32)
        for k, rim in enumerate(rims):
            source = me ^ k
            above = jnp.where(source == count - 1, rim[c], above)
            below = jnp.where(source == 0, rim[c], below)
        edges = jnp.concatenate([above, below], axis=0).astype(BF16)
        if strip % 16 == 0:
            for k, part in enumerate(parts):
                place(c, part[c], k * strip)
        else:
            body = jnp.concatenate([part[c].astype(F32) for part in parts], axis=0)
            place(c, body.astype(BF16), 0)
        place(c, edges, count * strip)


def assemble(me, parts, ranges, count):
    _, strip, broad = parts[0].shape
    tall = count * strip + 2 * RIM
    outs = [jax.ShapeDtypeStruct((high - low, tall, broad), BF16) for low, high in ranges]
    return pl.pallas_call(
        functools.partial(assemble_kernel, count, ranges),
        in_specs=[SMEM] + [VMEM] * count,
        out_specs=[VMEM] * len(outs),
        out_shape=outs,
        compiler_params=params(16),
        cost_estimate=cost(outs[0].size, 8 * outs[0].size),
        name="assemble_tile",
    )(me, *parts)


def smooth_planes(sources, down, across, middle, out):
    tall = down.shape[0] // KERNELS
    broad = sources[0].shape[2]
    half = broad // 2
    at = 0
    for source in sources:
        for c in range(source.shape[0]):
            found = jnp.dot(down[...], source[c], preferred_element_type=F32).astype(BF16)
            for k in range(KERNELS):
                middle[k, at * tall : (at + 1) * tall] = found[k * tall : (k + 1) * tall]
            at += 1
    chunks = -(-at // 4)
    sizes = [at // chunks + (i < at % chunks) for i in range(chunks)]
    for k in range(KERNELS):
        start = 0
        for size in sizes:
            rows = slice(start * tall, (start + size) * tall)
            quarter = half // 2
            left = jnp.dot(middle[k, rows, :half], across[k, 0], preferred_element_type=F32)
            right = jnp.dot(middle[k, rows, half:], across[k, 1], preferred_element_type=F32)
            seam = jnp.dot(
                middle[k, rows, quarter : quarter + half], across[k, 2], preferred_element_type=F32
            )
            parts = [
                left[:, :quarter],
                left[:, quarter:] + seam[:, :quarter],
                right[:, :quarter] + seam[:, quarter:],
                right[:, quarter:],
            ]
            for i, part in enumerate(parts):
                lanes = slice(i * quarter, (i + 1) * quarter)
                value = part.astype(BF16).reshape(size, tall, quarter)
                out[k, start : start + size, :, lanes] = value
            start += size


def smooth_kernel(inputs, me_ref, down, across, *refs):
    sources, (out, middle) = refs[:inputs], refs[inputs:]
    smooth_planes(sources, down.at[me_ref[0]], across, middle, out)


def smooth(me, sources, down, across, name):
    planes = sum(source.shape[0] for source in sources)
    broad = sources[0].shape[2]
    tall = down.shape[1] // KERNELS
    out = jax.ShapeDtypeStruct((KERNELS, planes, tall, broad), BF16)
    return pl.pallas_call(
        functools.partial(smooth_kernel, len(sources)),
        in_specs=[SMEM] + [VMEM] * (2 + len(sources)),
        out_specs=VMEM,
        out_shape=out,
        scratch_shapes=[pltpu.VMEM((KERNELS, planes * tall, broad), BF16)],
        compiler_params=params(20),
        cost_estimate=cost(2 * out.size * (broad + 256), 4 * out.size),
        name=name,
    )(me, down, across, *sources)


def boxcars(load, channels):
    x, two, four, eight, one, three = {}, {}, {}, {}, {}, {}
    for i in range(channels + 2 * EDGE):
        x[i] = load(i)
        if i >= 1:
            two[i - 1] = x[i - 1] + x[i]
        if i >= 3:
            four[i - 3] = two[i - 3] + two[i - 1]
        if i >= 7:
            eight[i - 7] = four[i - 7] + four[i - 3]
        if i >= 2:
            one[i - 1] = two[i - 2] + x[i]
        if i >= 6:
            three[i - 3] = four[i - 6] + one[i - 1]
        ready = [(0, i, x), (1, i - 1, one), (2, i - 3, three)]
        for w, center, table in ready:
            if EDGE <= center < EDGE + channels:
                yield w, center - EDGE, table[center]
        if i >= 2 * EDGE:
            yield 3, i - 2 * EDGE, eight[i - 14] + three[i - 3]


def layer_order(counts):
    own, halo = counts
    groups = len(own)
    order = []
    for g in range(groups):
        order += [(groups + g, c) for c in range(halo[g][0])]
    for g in range(groups):
        order += [(g, c) for c in range(own[g])]
    for g in range(groups):
        order += [(groups + g, halo[g][0] + c) for c in range(halo[g][1])]
    return order


def power_kernel(order, channels, inputs, me_ref, down, across, *refs):
    sources, ready = refs[:inputs], refs[inputs:-4]
    halo, power, middle, sums = refs[-4:]
    smooth_planes(sources, down.at[me_ref[0]], across, middle, halo)
    layers = list(ready) + [halo]
    tall, broad = halo.shape[2:]
    sums[...] = jnp.zeros_like(sums)
    lane_groups = broad // LANES

    def add(step, _):
        rows = pl.ds(pl.multiple_of(step // lane_groups * 16, 16), 16)
        lanes = pl.ds(pl.multiple_of(step % lane_groups * LANES, LANES), LANES)
        for k in range(KERNELS):

            def load(i, k=k):
                array, plane = order[i]
                return layers[array][k, plane, rows, lanes].astype(F32)

            for w, c, value in boxcars(load, channels):
                square = value * value
                sums[(k * WIDTHS + w) * channels + c] += square[:8] + square[8:]
        return 0

    lax.fori_loop(0, tall // 16 * lane_groups, add, 0)
    total = jnp.sum(jnp.sum(sums[...], axis=1), axis=1, keepdims=True)
    power[...] = jnp.broadcast_to(total, power.shape)


def smooth_power(me, sources, ready, order, channels, down, across):
    planes = sum(source.shape[0] for source in sources)
    _, _, tall, broad = ready[0].shape
    pairs = KERNELS * WIDTHS * channels
    halo = jax.ShapeDtypeStruct((KERNELS, planes, tall, broad), BF16)
    return pl.pallas_call(
        functools.partial(power_kernel, order, channels, len(sources)),
        in_specs=[SMEM] + [VMEM] * (2 + len(sources) + len(ready)),
        out_specs=[VMEM] * 2,
        out_shape=[halo, jax.ShapeDtypeStruct((pairs, LANES), F32)],
        scratch_shapes=[
            pltpu.VMEM((KERNELS, planes * tall, broad), BF16),
            pltpu.VMEM((pairs, 8, LANES), F32),
        ],
        compiler_params=params(32),
        cost_estimate=cost(2 * halo.size * (broad + 256), 8 * halo.size),
        name="smooth_power",
    )(me, down, across, *sources, *ready)


def score_kernel(order, count, cells, inputs, *refs):
    layers, clips, powers = refs[:inputs], refs[inputs], refs[inputs + 1 : inputs + 1 + count]
    out, factor = refs[-2:]
    channels, step_rows, broad = out.shape

    @pl.when(pl.program_id(0) == 0)
    def _():
        total = powers[0][...]
        for item in powers[1:]:
            total = total + item[...]
        scale = 10.0 / (clips[...] * jnp.sqrt(total / cells + EPSILON))
        factor[...] = jnp.broadcast_to(scale[:, None], factor.shape)

    lane_groups = broad // LANES
    base = pl.program_id(0) * step_rows

    def score(step, _):
        start = pl.multiple_of(step // lane_groups * 16, 16)
        rows = pl.ds(pl.multiple_of(base + start, 16), 16)
        lanes = pl.ds(pl.multiple_of(step % lane_groups * LANES, LANES), LANES)
        for half in range(2):
            best = [None] * channels
            for k in range(KERNELS):

                def load(i, k=k):
                    array, plane = order[i]
                    value = layers[array][k, plane, rows, lanes].astype(F32)
                    return value[half * 8 : half * 8 + 8]

                for w, c, value in boxcars(load, channels):
                    value = jnp.abs(value) * factor[(k * WIDTHS + w) * channels + c]
                    best[c] = value if best[c] is None else jnp.maximum(best[c], value)
            for c in range(channels):
                out[c, pl.ds(start + half * 8, 8), lanes] = best[c]
        return 0

    lax.fori_loop(0, step_rows // 16 * lane_groups, score, 0)


def score(layers, order, channels, clips, powers, cells):
    _, _, tall, broad = layers[0].shape
    pairs = KERNELS * WIDTHS * channels
    step = 32
    return pl.pallas_call(
        functools.partial(score_kernel, order, len(powers), cells, len(layers)),
        grid=(tall // step,),
        in_specs=[VMEM] * (len(layers) + 1 + len(powers)),
        out_specs=pl.BlockSpec((channels, step, broad), lambda i: (0, i, 0)),
        out_shape=jax.ShapeDtypeStruct((channels, tall, broad), F32),
        scratch_shapes=[pltpu.VMEM((pairs, 8, LANES), F32)],
        compiler_params=params(24),
        cost_estimate=cost(40 * KERNELS * channels * tall * broad, 8 * layers[0].size),
        name="score_cells",
    )(*layers, clips, *powers)


def shards(across_table, down_table, pieces, beam, destination, clip_tenths):
    count = lax.axis_size("sky")
    links = lax.axis_size("freq")
    piece_count, channels = pieces.shape[:2]
    groups = 2
    size = channels // groups
    me = lax.axis_index("sky").astype(jnp.int32).reshape(1)
    across = jnp.asarray(across_table)
    down = jnp.asarray(down_table)
    upward = [(i, i + 1) for i in range(links - 1)]
    downward = [(i + 1, i) for i in range(links - 1)]
    packed = pack(me, destination, pieces, beam, count, groups)
    arrived = [[part[0]] + [exchange(part[k], "sky", k) for k in range(1, count)] for part in packed]
    known = None
    own, halo = [], []
    for g in range(groups):
        strips, known = combine(me, known, arrived[g], size, piece_count, count)
        tiles = [strips[0]] + [exchange(strips[k], "sky", k) for k in range(1, count)]
        lower = (0, min(size, EDGE - g * size))
        upper = (max(0, channels - EDGE - g * size), size)
        cuts = [(0, size)] + [cut for cut in (lower, upper) if cut != (0, size)]
        parts = dict(zip(cuts, assemble(me, tiles, cuts, count)))
        low = lax.ppermute(parts[upper], "freq", upward)
        high = lax.ppermute(parts[lower], "freq", downward)
        own.append(parts[(0, size)])
        halo.append([low, high])
    order = layer_order(
        ([item.shape[0] for item in own], [[item.shape[0] for item in pair] for pair in halo])
    )
    ready = [smooth(me, [item], down, across, "smooth_own") for item in own]
    ready += [smooth(me, pair, down, across, "smooth_halo") for pair in halo[:-1]]
    last, power = smooth_power(me, halo[-1], ready, order, channels, down, across)
    powers = [power] + [exchange(power, "sky", k) for k in range(1, count)]
    clips = jnp.repeat(clip_tenths.astype(F32).reshape(-1), channels)
    clips = jnp.broadcast_to(clips[:, None], power.shape)
    cells = float(count * ROWB * LANES * COLB * LANES)
    return score(ready + [last], order, channels, clips, powers, cells)


def solution(mesh):
    count = mesh.shape["sky"]
    body = functools.partial(
        shards, across_matrices(COLB * LANES), down_matrices(count, ROWB * LANES // count)
    )
    return jax.shard_map(
        body,
        mesh=mesh,
        in_specs=(P("sky", "freq", None, None), P("sky", None, None), P("sky"), P()),
        out_specs=P("freq", "sky", None),
        check_vma=False,
    )
```

```python
import functools

import jax
import jax.numpy as jnp
import ml_dtypes
import numpy as np
from jax import lax
from jax.experimental import pallas as pl
from jax.experimental.pallas import tpu as pltpu
from jax.sharding import PartitionSpec as P

ROWB = 1
COLB = 4
RIM = 8
EDGE = 7
KERNELS = 3
WIDTHS = 4

REGULARIZER = 0.05
EPSILON = 1e-06
KERNEL_FWHM = (3.0, 6.0, 9.0)
HALF_WIDTHS = (0, 1, 3, 7)

LANES = 128
MIB = 1 << 20
F32 = jnp.float32
BF16 = jnp.bfloat16
SMEM = pl.BlockSpec(memory_space=pltpu.SMEM)
VMEM = pl.BlockSpec(memory_space=pltpu.VMEM)


def params(mib):
    return pltpu.CompilerParams(vmem_limit_bytes=mib * MIB)


def cost(flops, moved):
    return pl.CostEstimate(flops=int(flops), bytes_accessed=int(moved), transcendentals=0)


def tap_table(distance):
    offsets = np.arange(-RIM, RIM + 1).astype(np.float32)
    near = np.abs(distance) <= RIM
    index = np.clip(distance + RIM, 0, 2 * RIM)
    found = []
    for fwhm in KERNEL_FWHM:
        sigma = np.float32(fwhm / 2.3548)
        taps = np.exp(-offsets * offsets / (np.float32(2.0) * sigma * sigma)).astype(ml_dtypes.bfloat16)
        found.append(np.where(near, taps[index], np.zeros((), ml_dtypes.bfloat16)))
    return np.stack(found)


def across_matrices(broad):
    half = broad // 2
    cells = np.arange(broad)
    table = tap_table(cells[:, None] - cells[None, :])
    middle = slice(half // 2, half // 2 + half)
    seam = (cells[middle, None] < half) != (cells[None, middle] < half)
    crossing = np.where(seam[None], table[:, middle, middle], np.zeros((), ml_dtypes.bfloat16))
    return np.stack([table[:, :half, :half], table[:, half:, half:], crossing], axis=1)


def down_matrices(count, strip):
    tall = count * strip
    found = []
    for me in range(count):
        rows = [(me ^ k) * strip + np.arange(strip) for k in range(count)]
        rows += [np.arange(-RIM, 0), np.arange(tall, tall + RIM)]
        rows = np.concatenate(rows)
        found.append(tap_table(rows[None, :] - np.arange(tall)[:, None]).reshape(KERNELS * tall, tall + 2 * RIM))
    return np.stack(found)


def exchange(block, axis, k):
    count = lax.axis_size(axis)
    return lax.ppermute(block, axis, [(i, i ^ k) for i in range(count)])


def fetch_strip(pieces_hbm, beam_hbm, pieces, beams, sems, target):
    return (
        pltpu.make_async_copy(beam_hbm.at[:, target], beams, sems.at[0]),
        pltpu.make_async_copy(pieces_hbm.at[:, :, target], pieces, sems.at[1]),
    )


def weigh(pieces, beams, p):
    wide = beams[p].astype(F32)
    return [(wide * pieces[p, c].astype(F32)).astype(BF16) for c in range(pieces.shape[1])]


def pack_kernel(count, me_ref, owner_ref, pieces_hbm, beam_hbm, *refs):
    outs, (pieces, beams, packed, in_sems, out_sems) = refs[: count - 1], refs[count - 1 :]
    _, piece_count, channels, strip, _ = pieces.shape
    planes = channels + 1
    me = me_ref[0]

    def fetch(k):
        here = (pieces.at[k - 1], beams.at[k - 1], in_sems.at[k - 1])
        return fetch_strip(pieces_hbm, beam_hbm, *here, me ^ k)

    order = range(count - 1, 0, -1)
    for k in order:
        for copy in fetch(k):
            copy.start()
    row = lax.broadcasted_iota(jnp.int32, (strip, LANES), 0)
    plane = jnp.zeros((strip, LANES), jnp.int32)
    for p in range(piece_count):
        plane = jnp.where(row == p, owner_ref[p], plane)
    plane = plane.astype(F32).astype(BF16)
    for k in order:
        for copy in fetch(k):
            copy.wait()
        for p in range(piece_count):
            for c, value in enumerate(weigh(pieces.at[k - 1], beams.at[k - 1], p)):
                packed[k - 1, p * planes + c] = value
            packed[k - 1, p * planes + channels] = beams[k - 1, p]
        packed[k - 1, piece_count * planes] = plane
        pltpu.make_async_copy(packed.at[k - 1], outs[k - 1], out_sems.at[k - 1]).start()
    for k in order:
        pltpu.make_async_copy(packed.at[k - 1], outs[k - 1], out_sems.at[k - 1]).wait()


def pack(me, destination, parts, beams):
    piece_count, channels, count, strip, _ = parts.shape
    out = jax.ShapeDtypeStruct((piece_count * (channels + 1) + 1, strip, LANES), BF16)
    far = pl.BlockSpec(memory_space=pl.ANY)
    return pl.pallas_call(
        functools.partial(pack_kernel, count),
        in_specs=[SMEM, SMEM, far, far],
        out_specs=[far] * (count - 1),
        out_shape=[out] * (count - 1),
        scratch_shapes=[
            pltpu.VMEM((count - 1, piece_count, channels, strip, LANES), BF16),
            pltpu.VMEM((count - 1, piece_count, strip, LANES), BF16),
            pltpu.VMEM((count - 1,) + out.shape, BF16),
            pltpu.SemaphoreType.DMA((count - 1, 2)),
            pltpu.SemaphoreType.DMA((count - 1,)),
        ],
        compiler_params=params(58),
        cost_estimate=cost(parts.size, 4 * parts.size),
        name="pack_pieces",
    )(me, destination, parts, beams)


def gather_kernel(me_ref, owner_ref, pieces_hbm, beam_hbm, total, cover, pieces, beams, sems):
    copies = fetch_strip(pieces_hbm, beam_hbm, pieces, beams, sems, me_ref[0])
    for copy in copies:
        copy.start()
    total[...] = jnp.zeros_like(total)
    cover[...] = jnp.full(cover.shape, REGULARIZER, F32)
    for copy in copies:
        copy.wait()
    for p in range(pieces.shape[0]):
        block = owner_ref[p]
        beam = beams[p].astype(F32)
        cover[block] += beam * beam
        for c, value in enumerate(weigh(pieces, beams, p)):
            total[block, c] += value.astype(F32)


def gather_own(me, destination, parts, beams):
    piece_count, channels, count, strip, _ = parts.shape
    blocks = count * COLB
    far = pl.BlockSpec(memory_space=pl.ANY)
    return pl.pallas_call(
        gather_kernel,
        in_specs=[SMEM, SMEM, far, far],
        out_specs=[VMEM] * 2,
        out_shape=[
            jax.ShapeDtypeStruct((blocks, channels, strip, LANES), F32),
            jax.ShapeDtypeStruct((blocks, strip, LANES), F32),
        ],
        scratch_shapes=[
            pltpu.VMEM((piece_count, channels, strip, LANES), BF16),
            pltpu.VMEM((piece_count, strip, LANES), BF16),
            pltpu.SemaphoreType.DMA((2,)),
        ],
        compiler_params=params(24),
        cost_estimate=cost(parts.size, 4 * parts.size),
        name="gather_own",
    )(me, destination, parts, beams)


def write_strips(count, me, scale, total, outs):
    _, channels, strip, _ = total.shape
    first = me == 0
    last = me == count - 1
    for k, out in enumerate(outs):
        tile = me ^ k
        other = jnp.where(last, tile - 1, tile + 1)
        valid = jnp.logical_or(
            jnp.logical_and(last, tile > 0), jnp.logical_and(first, tile < count - 1)
        )
        other = jnp.clip(other, 0, count - 1)
        for column in range(COLB):
            lanes = slice(column * LANES, (column + 1) * LANES)
            block = tile * COLB + column
            factor = scale[block]
            for c in range(channels):
                out[c, :, lanes] = (total[block, c] * factor).astype(BF16)
            if out.shape[0] == channels:
                continue
            block = other * COLB + column
            rows = []
            for c in range(channels):
                high = total[block, c, strip - RIM :] * scale[block, strip - RIM :]
                low = total[block, c, :RIM] * scale[block, :RIM]
                rows.append(jnp.where(valid, jnp.where(last, high, low), 0.0))
            rims = jnp.concatenate(rows, axis=0)
            for e in range(channels * RIM // strip):
                out[channels + e, :, lanes] = rims[e * strip : (e + 1) * strip].astype(BF16)


def combine_kernel(count, piece_count, me_ref, total_in, cover_in, *refs):
    parts, outs = refs[: count - 1], refs[count - 1 : 2 * count - 1]
    total, cover, rows, table, sem = refs[2 * count - 1 :]
    planes = (parts[0].shape[0] - 1) // piece_count
    channels = planes - 1
    for i, part in enumerate(parts):
        plane = part[part.shape[0] - 1].astype(F32)[:piece_count]
        rows[i * piece_count : (i + 1) * piece_count] = plane.astype(jnp.int32)
    copy = pltpu.make_async_copy(rows, table, sem)
    copy.start()
    total[...] = total_in[...]
    cover[...] = cover_in[...]
    copy.wait()
    for i, part in enumerate(parts):

        def add(p, _, i=i, part=part):
            block = table[i * piece_count + p, 0]
            beam = part[p * planes + channels].astype(F32)
            cover[block] += beam * beam
            total[block] += part[pl.ds(p * planes, channels)].astype(F32)
            return 0

        lax.fori_loop(0, piece_count, add, 0)
    cover[...] = 1.0 / cover[...]
    write_strips(count, me_ref[0], cover, total, outs)


def combine(me, total, cover, parts, piece_count):
    count = len(parts) + 1
    blocks, channels, strip, _ = total.shape
    rim_planes = channels * RIM // strip
    outs = [
        jax.ShapeDtypeStruct((channels + rim_planes * (k != count - 1), strip, COLB * LANES), BF16)
        for k in range(count)
    ]
    rows = len(parts) * piece_count
    return pl.pallas_call(
        functools.partial(combine_kernel, count, piece_count),
        in_specs=[SMEM] + [VMEM] * (2 + len(parts)),
        out_specs=[VMEM] * count,
        out_shape=outs,
        scratch_shapes=[
            pltpu.VMEM(total.shape, F32),
            pltpu.VMEM(cover.shape, F32),
            pltpu.VMEM((rows, LANES), jnp.int32),
            pltpu.SMEM((rows, LANES), jnp.int32),
            pltpu.SemaphoreType.DMA,
        ],
        compiler_params=params(20),
        cost_estimate=cost(1, 1),
        name="combine_strips",
    )(me, total, cover, *parts)


def tile_plane(me, strips, channels, c):
    count = len(strips)
    strip, broad = strips[0].shape[1:]
    above = jnp.zeros((RIM, broad), F32)
    below = jnp.zeros((RIM, broad), F32)
    plane, row = divmod(c * RIM, strip)
    for k, part in enumerate(strips[:-1]):
        rim = part[channels + plane].astype(F32)[row : row + RIM]
        source = me ^ k
        above = jnp.where(source == count - 1, rim, above)
        below = jnp.where(source == 0, rim, below)
    if strip % 16 == 0:
        edges = jnp.concatenate([above, below], axis=0).astype(BF16)
        return jnp.concatenate([part[c] for part in strips] + [edges], axis=0)
    wide = [part[c].astype(F32) for part in strips]
    return jnp.concatenate(wide + [above, below], axis=0).astype(BF16)


def smooth_planes(me, strips, chosen, down, across, middle, out, base):
    tall = down.shape[0] // KERNELS
    broad = strips[0].shape[2]
    channels = strips[-1].shape[0]
    half = broad // 2
    at = len(chosen)
    for i, c in enumerate(chosen):
        plane = tile_plane(me, strips, channels, c)
        found = jnp.dot(down[...], plane, preferred_element_type=F32).astype(BF16)
        for k in range(KERNELS):
            middle[k, i * tall : (i + 1) * tall] = found[k * tall : (k + 1) * tall]
    chunks = -(-at // 4)
    sizes = [at // chunks + (i < at % chunks) for i in range(chunks)]
    for k in range(KERNELS):
        start = 0
        for size in sizes:
            rows = slice(start * tall, (start + size) * tall)
            quarter = half // 2
            left = jnp.dot(middle[k, rows, :half], across[k, 0], preferred_element_type=F32)
            right = jnp.dot(middle[k, rows, half:], across[k, 1], preferred_element_type=F32)
            seam = jnp.dot(
                middle[k, rows, quarter : quarter + half], across[k, 2], preferred_element_type=F32
            )
            parts = [
                left[:, :quarter],
                left[:, quarter:] + seam[:, :quarter],
                right[:, :quarter] + seam[:, quarter:],
                right[:, quarter:],
            ]
            for i, part in enumerate(parts):
                lanes = slice(i * quarter, (i + 1) * quarter)
                value = part.astype(BF16).reshape(size, tall, quarter)
                out[k, base + start : base + start + size, :, lanes] = value
            start += size


def smooth_kernel(count, me_ref, down, across, *refs):
    strips, (out, middle) = refs[:count], refs[count:]
    me = me_ref[0]
    smooth_planes(me, strips, range(out.shape[1]), down.at[me], across, middle, out, 0)


def smooth(me, strips, down, across):
    channels = strips[-1].shape[0]
    broad = strips[0].shape[2]
    tall = down.shape[1] // KERNELS
    out = jax.ShapeDtypeStruct((KERNELS, channels, tall, broad), BF16)
    return pl.pallas_call(
        functools.partial(smooth_kernel, len(strips)),
        in_specs=[SMEM] + [VMEM] * (2 + len(strips)),
        out_specs=VMEM,
        out_shape=out,
        scratch_shapes=[pltpu.VMEM((KERNELS, channels * tall, broad), BF16)],
        compiler_params=params(16),
        cost_estimate=cost(2 * out.size * (broad + 256), 4 * out.size),
        name="smooth_own",
    )(me, down, across, *strips)


def boxcars(load, channels):
    x, two, four, eight, one, three = {}, {}, {}, {}, {}, {}
    for i in range(channels + 2 * EDGE):
        x[i] = load(i)
        if i >= 1:
            two[i - 1] = x[i - 1] + x[i]
        if i >= 3:
            four[i - 3] = two[i - 3] + two[i - 1]
        if i >= 7:
            eight[i - 7] = four[i - 7] + four[i - 3]
        if i >= 2:
            one[i - 1] = two[i - 2] + x[i]
        if i >= 6:
            three[i - 3] = four[i - 6] + one[i - 1]
        ready = [(0, i, x), (1, i - 1, one), (2, i - 3, three)]
        for w, center, table in ready:
            if EDGE <= center < EDGE + channels:
                yield w, center - EDGE, table[center]
        if i >= 2 * EDGE:
            yield 3, i - 2 * EDGE, eight[i - 14] + three[i - 3]


def layer_order(channels):
    order = [(1, c) for c in range(EDGE)]
    order += [(0, c) for c in range(channels)]
    order += [(1, c) for c in range(EDGE, 2 * EDGE)]
    return order


def power_kernel(count, me_ref, down, across, own, *refs):
    low, high = refs[:count], refs[count : 2 * count]
    halo, power, middle, sums = refs[2 * count :]
    channels, tall, broad = own.shape[1:]
    me = me_ref[0]
    smooth_planes(me, low, range(channels - EDGE, channels), down.at[me], across, middle, halo, 0)
    smooth_planes(me, high, range(EDGE), down.at[me], across, middle, halo, EDGE)
    layers = (own, halo)
    order = layer_order(channels)
    sums[...] = jnp.zeros_like(sums)
    lane_groups = broad // LANES

    def add(step, _):
        rows = pl.ds(pl.multiple_of(step // lane_groups * 16, 16), 16)
        lanes = pl.ds(pl.multiple_of(step % lane_groups * LANES, LANES), LANES)
        for k in range(KERNELS):

            def load(i, k=k):
                array, plane = order[i]
                return layers[array][k, plane, rows, lanes].astype(F32)

            for w, c, value in boxcars(load, channels):
                square = value * value
                sums[(k * WIDTHS + w) * channels + c] += square[:8] + square[8:]
        return 0

    lax.fori_loop(0, tall // 16 * lane_groups, add, 0)
    total = jnp.sum(jnp.sum(sums[...], axis=1), axis=1, keepdims=True)
    power[...] = jnp.broadcast_to(total, power.shape)


def smooth_power(me, own, low, high, down, across):
    _, channels, tall, broad = own.shape
    pairs = KERNELS * WIDTHS * channels
    halo = jax.ShapeDtypeStruct((KERNELS, 2 * EDGE, tall, broad), BF16)
    return pl.pallas_call(
        functools.partial(power_kernel, len(low)),
        in_specs=[SMEM] + [VMEM] * (3 + len(low) + len(high)),
        out_specs=[VMEM] * 2,
        out_shape=[halo, jax.ShapeDtypeStruct((pairs, LANES), F32)],
        scratch_shapes=[
            pltpu.VMEM((KERNELS, EDGE * tall, broad), BF16),
            pltpu.VMEM((pairs, 8, LANES), F32),
        ],
        compiler_params=params(24),
        cost_estimate=cost(2 * halo.size * (broad + 256), 8 * halo.size),
        name="smooth_power",
    )(me, down, across, own, *low, *high)


def score_kernel(count, cells, own, halo, clips, *refs):
    layers, powers = (own, halo), refs[:count]
    out, factor = refs[-2:]
    channels, step_rows, broad = out.shape
    order = layer_order(channels)

    @pl.when(pl.program_id(0) == 0)
    def _():
        total = powers[0][...]
        for item in powers[1:]:
            total = total + item[...]
        scale = 10.0 / (clips[...] * jnp.sqrt(total / cells + EPSILON))
        factor[...] = jnp.broadcast_to(scale[:, None], factor.shape)

    lane_groups = broad // LANES
    base = pl.program_id(0) * step_rows

    def score(step, _):
        start = pl.multiple_of(step // lane_groups * 16, 16)
        rows = pl.ds(pl.multiple_of(base + start, 16), 16)
        lanes = pl.ds(pl.multiple_of(step % lane_groups * LANES, LANES), LANES)
        for half in range(2):
            best = [None] * channels
            for k in range(KERNELS):

                def load(i, k=k):
                    array, plane = order[i]
                    value = layers[array][k, plane, rows, lanes].astype(F32)
                    return value[half * 8 : half * 8 + 8]

                for w, c, value in boxcars(load, channels):
                    value = jnp.abs(value) * factor[(k * WIDTHS + w) * channels + c]
                    best[c] = value if best[c] is None else jnp.maximum(best[c], value)
            for c in range(channels):
                out[c, pl.ds(start + half * 8, 8), lanes] = best[c]
        return 0

    lax.fori_loop(0, step_rows // 16 * lane_groups, score, 0)


def score(own, halo, clips, powers, cells):
    _, channels, tall, broad = own.shape
    pairs = KERNELS * WIDTHS * channels
    step = 32
    return pl.pallas_call(
        functools.partial(score_kernel, len(powers), cells),
        grid=(tall // step,),
        in_specs=[VMEM] * (3 + len(powers)),
        out_specs=pl.BlockSpec((channels, step, broad), lambda i: (0, i, 0)),
        out_shape=jax.ShapeDtypeStruct((channels, tall, broad), F32),
        scratch_shapes=[pltpu.VMEM((pairs, 8, LANES), F32)],
        compiler_params=params(14),
        cost_estimate=cost(40 * KERNELS * channels * tall * broad, 8 * own.size),
        name="score_cells",
    )(own, halo, clips, *powers)


def shards(across_table, down_table, pieces, beam, destination, clip_tenths):
    count = lax.axis_size("sky")
    links = lax.axis_size("freq")
    piece_count, channels = pieces.shape[:2]
    me = lax.axis_index("sky").astype(jnp.int32).reshape(1)
    across = jnp.asarray(across_table)
    down = jnp.asarray(down_table)

    def neighbours(block):
        low = lax.ppermute(block, "freq", [(i, i + 1) for i in range(links - 1)])
        high = lax.ppermute(block, "freq", [(i + 1, i) for i in range(links - 1)])
        return low, high

    strip = LANES // count
    parts = pieces.reshape(piece_count, channels, count, strip, LANES)
    beams = beam.reshape(piece_count, count, strip, LANES)
    packed = pack(me, destination, parts, beams)
    arrived = [exchange(block, "sky", k) for k, block in enumerate(packed, 1)]
    total, cover = gather_own(me, destination, parts, beams)
    strips = combine(me, total, cover, arrived, piece_count)
    last = count - 1
    halo = [neighbours(strips[0])]
    opposite, *halo[0] = lax.optimization_barrier((strips[last], *halo[0]))
    tiles = [strips[0]] + [exchange(strips[k], "sky", k) for k in range(1, last)]
    tiles.append(exchange(opposite, "sky", last))
    halo += [neighbours(tile) for tile in tiles[1:last]]
    flat = [block for pair in halo for block in pair]
    final, *flat = lax.optimization_barrier((tiles[last], *flat))
    halo = [flat[2 * k : 2 * k + 2] for k in range(last)] + [neighbours(final)]
    own = smooth(me, tiles, down, across)
    low, high = zip(*halo)
    sides, power = smooth_power(me, own, low, high, down, across)
    powers = [power] + [exchange(power, "sky", k) for k in range(1, count)]
    clips = jnp.repeat(clip_tenths.astype(F32).reshape(-1), channels)
    clips = jnp.broadcast_to(clips[:, None], power.shape)
    cells = float(count * ROWB * LANES * COLB * LANES)
    return score(own, sides, clips, powers, cells)


def solution(mesh):
    count = mesh.shape["sky"]
    body = functools.partial(
        shards, across_matrices(COLB * LANES), down_matrices(count, ROWB * LANES // count)
    )
    return jax.shard_map(
        body,
        mesh=mesh,
        in_specs=(P("sky", "freq", None, None), P("sky", None, None), P("sky"), P()),
        out_specs=P("freq", "sky", None),
        check_vma=False,
    )
```

```python
import functools

import jax
import jax.numpy as jnp
import ml_dtypes
import numpy as np
from jax import lax
from jax.experimental import pallas as pl
from jax.experimental.pallas import tpu as pltpu
from jax.sharding import PartitionSpec as P

ROWB = 1
COLB = 4
RIM = 8
EDGE = 7
KERNELS = 3
WIDTHS = 4

REGULARIZER = 0.05
EPSILON = 1e-06
KERNEL_FWHM = (3.0, 6.0, 9.0)
HALF_WIDTHS = (0, 1, 3, 7)

LANES = 128
MIB = 1 << 20
F32 = jnp.float32
BF16 = jnp.bfloat16
SMEM = pl.BlockSpec(memory_space=pltpu.SMEM)
VMEM = pl.BlockSpec(memory_space=pltpu.VMEM)


def params(mib):
    return pltpu.CompilerParams(vmem_limit_bytes=mib * MIB)


def cost(flops, moved):
    return pl.CostEstimate(flops=int(flops), bytes_accessed=int(moved), transcendentals=0)


def tap_table(distance):
    offsets = np.arange(-RIM, RIM + 1).astype(np.float32)
    near = np.abs(distance) <= RIM
    index = np.clip(distance + RIM, 0, 2 * RIM)
    found = []
    for fwhm in KERNEL_FWHM:
        sigma = np.float32(fwhm / 2.3548)
        taps = np.exp(-offsets * offsets / (np.float32(2.0) * sigma * sigma)).astype(ml_dtypes.bfloat16)
        found.append(np.where(near, taps[index], np.zeros((), ml_dtypes.bfloat16)))
    return np.stack(found)


def across_matrices(broad):
    half = broad // 2
    cells = np.arange(broad)
    table = tap_table(cells[:, None] - cells[None, :])
    middle = slice(half // 2, half // 2 + half)
    seam = (cells[middle, None] < half) != (cells[None, middle] < half)
    crossing = np.where(seam[None], table[:, middle, middle], np.zeros((), ml_dtypes.bfloat16))
    return np.stack([table[:, :half, :half], table[:, half:, half:], crossing], axis=1)


def down_matrices(count, strip):
    tall = count * strip
    found = []
    for me in range(count):
        rows = [(me ^ k) * strip + np.arange(strip) for k in range(count)]
        rows += [np.arange(-RIM, 0), np.arange(tall, tall + RIM)]
        rows = np.concatenate(rows)
        found.append(tap_table(rows[None, :] - np.arange(tall)[:, None]).reshape(KERNELS * tall, tall + 2 * RIM))
    return np.stack(found)


def exchange(block, axis, k):
    count = lax.axis_size(axis)
    return lax.ppermute(block, axis, [(i, i ^ k) for i in range(count)])


def fetch_strip(pieces_hbm, beam_hbm, pieces, beams, sems, target):
    return (
        pltpu.make_async_copy(beam_hbm.at[:, target], beams, sems.at[0]),
        pltpu.make_async_copy(pieces_hbm.at[:, :, target], pieces, sems.at[1]),
    )


def weigh(pieces, beams, p):
    wide = beams[p].astype(F32)
    return [(wide * pieces[p, c].astype(F32)).astype(BF16) for c in range(pieces.shape[1])]


def pack_kernel(count, me_ref, owner_ref, pieces_hbm, beam_hbm, *refs):
    outs, (pieces, beams, packed, in_sems, out_sems) = refs[: count - 1], refs[count - 1 :]
    _, piece_count, channels, strip, _ = pieces.shape
    planes = channels + 1
    me = me_ref[0]

    def fetch(k):
        here = (pieces.at[k - 1], beams.at[k - 1], in_sems.at[k - 1])
        return fetch_strip(pieces_hbm, beam_hbm, *here, me ^ k)

    order = range(count - 1, 0, -1)
    for k in order:
        for copy in fetch(k):
            copy.start()
    row = lax.broadcasted_iota(jnp.int32, (strip, LANES), 0)
    plane = jnp.zeros((strip, LANES), jnp.int32)
    for p in range(piece_count):
        plane = jnp.where(row == p, owner_ref[p], plane)
    plane = plane.astype(F32).astype(BF16)
    for k in order:
        for copy in fetch(k):
            copy.wait()
        for p in range(piece_count):
            for c, value in enumerate(weigh(pieces.at[k - 1], beams.at[k - 1], p)):
                packed[k - 1, p * planes + c] = value
            packed[k - 1, p * planes + channels] = beams[k - 1, p]
        packed[k - 1, piece_count * planes] = plane
        pltpu.make_async_copy(packed.at[k - 1], outs[k - 1], out_sems.at[k - 1]).start()
    for k in order:
        pltpu.make_async_copy(packed.at[k - 1], outs[k - 1], out_sems.at[k - 1]).wait()


def pack(me, destination, parts, beams):
    piece_count, channels, count, strip, _ = parts.shape
    out = jax.ShapeDtypeStruct((piece_count * (channels + 1) + 1, strip, LANES), BF16)
    far = pl.BlockSpec(memory_space=pl.ANY)
    return pl.pallas_call(
        functools.partial(pack_kernel, count),
        in_specs=[SMEM, SMEM, far, far],
        out_specs=[far] * (count - 1),
        out_shape=[out] * (count - 1),
        scratch_shapes=[
            pltpu.VMEM((count - 1, piece_count, channels, strip, LANES), BF16),
            pltpu.VMEM((count - 1, piece_count, strip, LANES), BF16),
            pltpu.VMEM((count - 1,) + out.shape, BF16),
            pltpu.SemaphoreType.DMA((count - 1, 2)),
            pltpu.SemaphoreType.DMA((count - 1,)),
        ],
        compiler_params=params(58),
        cost_estimate=cost(parts.size, 4 * parts.size),
        name="pack_pieces",
    )(me, destination, parts, beams)


def gather_kernel(me_ref, owner_ref, pieces_hbm, beam_hbm, total, cover, pieces, beams, sems):
    copies = fetch_strip(pieces_hbm, beam_hbm, pieces, beams, sems, me_ref[0])
    for copy in copies:
        copy.start()
    total[...] = jnp.zeros_like(total)
    cover[...] = jnp.full(cover.shape, REGULARIZER, F32)
    for copy in copies:
        copy.wait()
    for p in range(pieces.shape[0]):
        block = owner_ref[p]
        beam = beams[p].astype(F32)
        cover[block] += beam * beam
        for c, value in enumerate(weigh(pieces, beams, p)):
            total[block, c] += value.astype(F32)


def gather_own(me, destination, parts, beams):
    piece_count, channels, count, strip, _ = parts.shape
    blocks = count * COLB
    far = pl.BlockSpec(memory_space=pl.ANY)
    return pl.pallas_call(
        gather_kernel,
        in_specs=[SMEM, SMEM, far, far],
        out_specs=[VMEM] * 2,
        out_shape=[
            jax.ShapeDtypeStruct((blocks, channels, strip, LANES), F32),
            jax.ShapeDtypeStruct((blocks, strip, LANES), F32),
        ],
        scratch_shapes=[
            pltpu.VMEM((piece_count, channels, strip, LANES), BF16),
            pltpu.VMEM((piece_count, strip, LANES), BF16),
            pltpu.SemaphoreType.DMA((2,)),
        ],
        compiler_params=params(24),
        cost_estimate=cost(parts.size, 4 * parts.size),
        name="gather_own",
    )(me, destination, parts, beams)


def write_strips(count, me, scale, total, outs):
    _, channels, strip, _ = total.shape
    first = me == 0
    last = me == count - 1
    for k, out in enumerate(outs):
        tile = me ^ k
        other = jnp.where(last, tile - 1, tile + 1)
        valid = jnp.logical_or(
            jnp.logical_and(last, tile > 0), jnp.logical_and(first, tile < count - 1)
        )
        other = jnp.clip(other, 0, count - 1)
        for column in range(COLB):
            lanes = slice(column * LANES, (column + 1) * LANES)
            block = tile * COLB + column
            factor = scale[block]
            for c in range(channels):
                out[c, :, lanes] = (total[block, c] * factor).astype(BF16)
            if out.shape[0] == channels:
                continue
            block = other * COLB + column
            rows = []
            for c in range(channels):
                high = total[block, c, strip - RIM :] * scale[block, strip - RIM :]
                low = total[block, c, :RIM] * scale[block, :RIM]
                rows.append(jnp.where(valid, jnp.where(last, high, low), 0.0))
            rims = jnp.concatenate(rows, axis=0)
            for e in range(channels * RIM // strip):
                out[channels + e, :, lanes] = rims[e * strip : (e + 1) * strip].astype(BF16)


def combine_kernel(count, piece_count, me_ref, total_in, cover_in, *refs):
    parts, outs = refs[: count - 1], refs[count - 1 : 2 * count - 1]
    total, cover, rows, table, sem = refs[2 * count - 1 :]
    planes = (parts[0].shape[0] - 1) // piece_count
    channels = planes - 1
    for i, part in enumerate(parts):
        plane = part[part.shape[0] - 1].astype(F32)[:piece_count]
        rows[i * piece_count : (i + 1) * piece_count] = plane.astype(jnp.int32)
    copy = pltpu.make_async_copy(rows, table, sem)
    copy.start()
    total[...] = total_in[...]
    cover[...] = cover_in[...]
    copy.wait()
    for i, part in enumerate(parts):

        def add(p, _, i=i, part=part):
            block = table[i * piece_count + p, 0]
            beam = part[p * planes + channels].astype(F32)
            cover[block] += beam * beam
            total[block] += part[pl.ds(p * planes, channels)].astype(F32)
            return 0

        lax.fori_loop(0, piece_count, add, 0)
    cover[...] = 1.0 / cover[...]
    write_strips(count, me_ref[0], cover, total, outs)


def combine(me, total, cover, parts, piece_count):
    count = len(parts) + 1
    blocks, channels, strip, _ = total.shape
    rim_planes = channels * RIM // strip
    outs = [
        jax.ShapeDtypeStruct((channels + rim_planes * (k != count - 1), strip, COLB * LANES), BF16)
        for k in range(count)
    ]
    rows = len(parts) * piece_count
    return pl.pallas_call(
        functools.partial(combine_kernel, count, piece_count),
        in_specs=[SMEM] + [VMEM] * (2 + len(parts)),
        out_specs=[VMEM] * count,
        out_shape=outs,
        scratch_shapes=[
            pltpu.VMEM(total.shape, F32),
            pltpu.VMEM(cover.shape, F32),
            pltpu.VMEM((rows, LANES), jnp.int32),
            pltpu.SMEM((rows, LANES), jnp.int32),
            pltpu.SemaphoreType.DMA,
        ],
        compiler_params=params(20),
        cost_estimate=cost(1, 1),
        name="combine_strips",
    )(me, total, cover, *parts)


def edge_rows(me, strips, channels, c):
    count = len(strips) + 1
    strip, broad = strips[0].shape[1:]
    above = jnp.zeros((RIM, broad), F32)
    below = jnp.zeros((RIM, broad), F32)
    plane, row = divmod(c * RIM, strip)
    for k, part in enumerate(strips):
        rim = part[channels + plane].astype(F32)[row : row + RIM]
        source = me ^ k
        above = jnp.where(source == count - 1, rim, above)
        below = jnp.where(source == 0, rim, below)
    return [above, below]


def stack_rows(parts):
    if all(part.shape[0] % 16 == 0 for part in parts):
        return jnp.concatenate(parts, axis=0)
    return jnp.concatenate([part.astype(F32) for part in parts], axis=0).astype(BF16)


def join_kernel(me_ref, *refs):
    strips, (lower, upper) = refs[:-2], refs[-2:]
    me = me_ref[0]
    channels = strips[0].shape[0] - upper_rim_planes(strips[0].shape[1], strips[0].shape[0])
    for c in range(channels):
        edges = jnp.concatenate(edge_rows(me, strips, channels, c), axis=0).astype(BF16)
        plane = stack_rows([part[c] for part in strips] + [edges])
        if c < EDGE:
            lower[c] = plane
        if c >= channels - EDGE:
            upper[c - (channels - EDGE)] = plane


def upper_rim_planes(strip, planes):
    return planes * RIM // (strip + RIM)


def join(me, strips):
    _, strip, broad = strips[0].shape
    out = jax.ShapeDtypeStruct((EDGE, len(strips) * strip + 2 * RIM, broad), BF16)
    return pl.pallas_call(
        join_kernel,
        in_specs=[SMEM] + [VMEM] * len(strips),
        out_specs=[VMEM] * 2,
        out_shape=[out] * 2,
        compiler_params=params(16),
        cost_estimate=cost(1, 1),
        name="join_strips",
    )(me, *strips)


def smooth_planes(planes, down, across, middle, out, base):
    tall = down.shape[0] // KERNELS
    broad = across.shape[2] * 2
    half = broad // 2
    at = len(planes)
    for i, plane in enumerate(planes):
        found = jnp.dot(down[...], plane(), preferred_element_type=F32).astype(BF16)
        for k in range(KERNELS):
            middle[k, i * tall : (i + 1) * tall] = found[k * tall : (k + 1) * tall]
    chunks = -(-at // 4)
    sizes = [at // chunks + (i < at % chunks) for i in range(chunks)]
    for k in range(KERNELS):
        start = 0
        for size in sizes:
            rows = slice(start * tall, (start + size) * tall)
            quarter = half // 2
            left = jnp.dot(middle[k, rows, :half], across[k, 0], preferred_element_type=F32)
            right = jnp.dot(middle[k, rows, half:], across[k, 1], preferred_element_type=F32)
            seam = jnp.dot(
                middle[k, rows, quarter : quarter + half], across[k, 2], preferred_element_type=F32
            )
            parts = [
                left[:, :quarter],
                left[:, quarter:] + seam[:, :quarter],
                right[:, :quarter] + seam[:, quarter:],
                right[:, quarter:],
            ]
            for i, part in enumerate(parts):
                lanes = slice(i * quarter, (i + 1) * quarter)
                value = part.astype(BF16).reshape(size, tall, quarter)
                out[k, base + start : base + start + size, :, lanes] = value
            start += size


def smooth_kernel(count, me_ref, down, across, *refs):
    strips, (out, middle) = refs[:count], refs[count:]
    me = me_ref[0]
    channels = out.shape[1]

    def plane(c):
        edges = jnp.concatenate(edge_rows(me, strips[:-1], channels, c), axis=0).astype(BF16)
        return stack_rows([part[c] for part in strips] + [edges])

    planes = [functools.partial(plane, c) for c in range(channels)]
    smooth_planes(planes, down.at[me], across, middle, out, 0)


def smooth(me, strips, down, across):
    channels = strips[-1].shape[0]
    broad = strips[0].shape[2]
    tall = down.shape[1] // KERNELS
    out = jax.ShapeDtypeStruct((KERNELS, channels, tall, broad), BF16)
    return pl.pallas_call(
        functools.partial(smooth_kernel, len(strips)),
        in_specs=[SMEM] + [VMEM] * (2 + len(strips)),
        out_specs=VMEM,
        out_shape=out,
        scratch_shapes=[pltpu.VMEM((KERNELS, channels * tall, broad), BF16)],
        compiler_params=params(16),
        cost_estimate=cost(2 * out.size * (broad + 256), 4 * out.size),
        name="smooth_own",
    )(me, down, across, *strips)


def boxcars(load, channels):
    x, two, four, eight, one, three = {}, {}, {}, {}, {}, {}
    for i in range(channels + 2 * EDGE):
        x[i] = load(i)
        if i >= 1:
            two[i - 1] = x[i - 1] + x[i]
        if i >= 3:
            four[i - 3] = two[i - 3] + two[i - 1]
        if i >= 7:
            eight[i - 7] = four[i - 7] + four[i - 3]
        if i >= 2:
            one[i - 1] = two[i - 2] + x[i]
        if i >= 6:
            three[i - 3] = four[i - 6] + one[i - 1]
        ready = [(0, i, x), (1, i - 1, one), (2, i - 3, three)]
        for w, center, table in ready:
            if EDGE <= center < EDGE + channels:
                yield w, center - EDGE, table[center]
        if i >= 2 * EDGE:
            yield 3, i - 2 * EDGE, eight[i - 14] + three[i - 3]


def layer_order(channels):
    order = [(1, c) for c in range(EDGE)]
    order += [(0, c) for c in range(channels)]
    order += [(1, c) for c in range(EDGE, 2 * EDGE)]
    return order


def power_kernel(me_ref, down, across, own, low, low_last, high, high_last, halo, power, middle, sums):
    channels, tall, broad = own.shape[1:]
    me = me_ref[0]
    for joined, last, first, base in (
        (low, low_last, channels - EDGE, 0),
        (high, high_last, 0, EDGE),
    ):

        def plane(c, joined=joined, last=last, first=first):
            rows = joined[c]
            body = rows.shape[0] - 2 * RIM
            if last.shape[1] % 16 == 0:
                return jnp.concatenate([rows[:body], last[first + c], rows[body:]], axis=0)
            rows = rows.astype(F32)
            middle_rows = last[first + c].astype(F32)
            return jnp.concatenate([rows[:body], middle_rows, rows[body:]], axis=0).astype(BF16)

        planes = [functools.partial(plane, c) for c in range(EDGE)]
        smooth_planes(planes, down.at[me], across, middle, halo, base)
    layers = (own, halo)
    order = layer_order(channels)
    sums[...] = jnp.zeros_like(sums)
    lane_groups = broad // LANES

    def add(step, _):
        rows = pl.ds(pl.multiple_of(step // lane_groups * 16, 16), 16)
        lanes = pl.ds(pl.multiple_of(step % lane_groups * LANES, LANES), LANES)
        for k in range(KERNELS):

            def load(i, k=k):
                array, plane = order[i]
                return layers[array][k, plane, rows, lanes].astype(F32)

            for w, c, value in boxcars(load, channels):
                square = value * value
                sums[(k * WIDTHS + w) * channels + c] += square[:8] + square[8:]
        return 0

    lax.fori_loop(0, tall // 16 * lane_groups, add, 0)
    total = jnp.sum(jnp.sum(sums[...], axis=1), axis=1, keepdims=True)
    power[...] = jnp.broadcast_to(total, power.shape)


def smooth_power(me, own, sides, down, across):
    _, channels, tall, broad = own.shape
    pairs = KERNELS * WIDTHS * channels
    halo = jax.ShapeDtypeStruct((KERNELS, 2 * EDGE, tall, broad), BF16)
    return pl.pallas_call(
        power_kernel,
        in_specs=[SMEM] + [VMEM] * (3 + len(sides)),
        out_specs=[VMEM] * 2,
        out_shape=[halo, jax.ShapeDtypeStruct((pairs, LANES), F32)],
        scratch_shapes=[
            pltpu.VMEM((KERNELS, EDGE * tall, broad), BF16),
            pltpu.VMEM((pairs, 8, LANES), F32),
        ],
        compiler_params=params(24),
        cost_estimate=cost(2 * halo.size * (broad + 256), 8 * halo.size),
        name="smooth_power",
    )(me, down, across, own, *sides)


def score_kernel(count, cells, own, halo, clips, *refs):
    layers, powers = (own, halo), refs[:count]
    out, factor = refs[-2:]
    channels, step_rows, broad = out.shape
    order = layer_order(channels)

    @pl.when(pl.program_id(0) == 0)
    def _():
        total = powers[0][...]
        for item in powers[1:]:
            total = total + item[...]
        noise = jnp.sqrt(total / cells + EPSILON)
        for k in range(KERNELS):
            for w in range(WIDTHS):
                rows = slice((k * WIDTHS + w) * channels, (k * WIDTHS + w + 1) * channels)
                scale = 10.0 / (clips[k, w].astype(F32) * noise[rows])
                factor[rows] = jnp.broadcast_to(scale[:, None], (channels,) + factor.shape[1:])

    lane_groups = broad // LANES
    base = pl.program_id(0) * step_rows

    def score(step, _):
        start = pl.multiple_of(step // lane_groups * 16, 16)
        rows = pl.ds(pl.multiple_of(base + start, 16), 16)
        lanes = pl.ds(pl.multiple_of(step % lane_groups * LANES, LANES), LANES)
        for half in range(2):
            best = [None] * channels
            for k in range(KERNELS):

                def load(i, k=k):
                    array, plane = order[i]
                    value = layers[array][k, plane, rows, lanes].astype(F32)
                    return value[half * 8 : half * 8 + 8]

                for w, c, value in boxcars(load, channels):
                    value = jnp.abs(value) * factor[(k * WIDTHS + w) * channels + c]
                    best[c] = value if best[c] is None else jnp.maximum(best[c], value)
            for c in range(channels):
                out[c, pl.ds(start + half * 8, 8), lanes] = best[c]
        return 0

    lax.fori_loop(0, step_rows // 16 * lane_groups, score, 0)


def score(own, halo, clips, powers, cells):
    _, channels, tall, broad = own.shape
    pairs = KERNELS * WIDTHS * channels
    step = 32
    return pl.pallas_call(
        functools.partial(score_kernel, len(powers), cells),
        grid=(tall // step,),
        in_specs=[VMEM, VMEM, SMEM] + [VMEM] * len(powers),
        out_specs=pl.BlockSpec((channels, step, broad), lambda i: (0, i, 0)),
        out_shape=jax.ShapeDtypeStruct((channels, tall, broad), F32),
        scratch_shapes=[pltpu.VMEM((pairs, 8, LANES), F32)],
        compiler_params=params(14),
        cost_estimate=cost(40 * KERNELS * channels * tall * broad, 8 * own.size),
        name="score_cells",
    )(own, halo, clips, *powers)


def shards(across_table, down_table, pieces, beam, destination, clip_tenths):
    count = lax.axis_size("sky")
    links = lax.axis_size("freq")
    piece_count, channels = pieces.shape[:2]
    me = lax.axis_index("sky").astype(jnp.int32).reshape(1)
    across = jnp.asarray(across_table)
    down = jnp.asarray(down_table)

    strip = LANES // count
    parts = pieces.reshape(piece_count, channels, count, strip, LANES)
    beams = beam.reshape(piece_count, count, strip, LANES)
    packed = pack(me, destination, parts, beams)
    arrived = [exchange(block, "sky", k) for k, block in enumerate(packed, 1)]
    total, cover = gather_own(me, destination, parts, beams)
    strips = combine(me, total, cover, arrived, piece_count)
    tiles = [strips[0]] + [exchange(strips[k], "sky", k) for k in range(1, count)]
    upward = [(i, i + 1) for i in range(links - 1)]
    downward = [(i + 1, i) for i in range(links - 1)]
    lower, upper = join(me, tiles[:-1])
    sides = [
        lax.ppermute(upper, "freq", upward),
        lax.ppermute(tiles[-1], "freq", upward),
        lax.ppermute(lower, "freq", downward),
        lax.ppermute(tiles[-1], "freq", downward),
    ]
    own = smooth(me, tiles, down, across)
    halo, power = smooth_power(me, own, sides, down, across)
    powers = [power] + [exchange(power, "sky", k) for k in range(1, count)]
    cells = float(count * ROWB * LANES * COLB * LANES)
    return score(own, halo, clip_tenths, powers, cells)


def solution(mesh):
    count = mesh.shape["sky"]
    body = functools.partial(
        shards, across_matrices(COLB * LANES), down_matrices(count, ROWB * LANES // count)
    )
    return jax.shard_map(
        body,
        mesh=mesh,
        in_specs=(P("sky", "freq", None, None), P("sky", None, None), P("sky"), P()),
        out_specs=P("freq", "sky", None),
        check_vma=False,
    )
```

```python
import functools

import jax
import jax.numpy as jnp
import ml_dtypes
import numpy as np
from jax import lax
from jax.experimental import pallas as pl
from jax.experimental.pallas import tpu as pltpu
from jax.sharding import PartitionSpec as P

ROWB = 1
COLB = 4
RIM = 8
EDGE = 7
KERNELS = 3
WIDTHS = 4

REGULARIZER = 0.05
EPSILON = 1e-06
KERNEL_FWHM = (3.0, 6.0, 9.0)
HALF_WIDTHS = (0, 1, 3, 7)

LANES = 128
MIB = 1 << 20
F32 = jnp.float32
BF16 = jnp.bfloat16
SMEM = pl.BlockSpec(memory_space=pltpu.SMEM)
VMEM = pl.BlockSpec(memory_space=pltpu.VMEM)


def params(mib):
    return pltpu.CompilerParams(vmem_limit_bytes=mib * MIB)


def cost(flops, moved):
    return pl.CostEstimate(flops=int(flops), bytes_accessed=int(moved), transcendentals=0)


def tap_table(distance):
    offsets = np.arange(-RIM, RIM + 1).astype(np.float32)
    near = np.abs(distance) <= RIM
    index = np.clip(distance + RIM, 0, 2 * RIM)
    found = []
    for fwhm in KERNEL_FWHM:
        sigma = np.float32(fwhm / 2.3548)
        taps = np.exp(-offsets * offsets / (np.float32(2.0) * sigma * sigma)).astype(ml_dtypes.bfloat16)
        found.append(np.where(near, taps[index], np.zeros((), ml_dtypes.bfloat16)))
    return np.stack(found)


def across_matrices(broad):
    half = broad // 2
    cells = np.arange(broad)
    table = tap_table(cells[:, None] - cells[None, :])
    middle = slice(half // 2, half // 2 + half)
    seam = (cells[middle, None] < half) != (cells[None, middle] < half)
    crossing = np.where(seam[None], table[:, middle, middle], np.zeros((), ml_dtypes.bfloat16))
    return np.stack([table[:, :half, :half], table[:, half:, half:], crossing], axis=1)


def down_matrices(count, strip):
    tall = count * strip
    found = []
    for me in range(count):
        rows = [(me ^ k) * strip + np.arange(strip) for k in range(count)]
        rows += [np.arange(-RIM, 0), np.arange(tall, tall + RIM)]
        rows = np.concatenate(rows)
        found.append(tap_table(rows[None, :] - np.arange(tall)[:, None]).reshape(KERNELS * tall, tall + 2 * RIM))
    return np.stack(found)


def exchange(block, axis, k):
    count = lax.axis_size(axis)
    return lax.ppermute(block, axis, [(i, i ^ k) for i in range(count)])


def fetch_strip(pieces_hbm, beam_hbm, pieces, beams, sems, target):
    return (
        pltpu.make_async_copy(beam_hbm.at[:, target], beams, sems.at[0]),
        pltpu.make_async_copy(pieces_hbm.at[:, :, target], pieces, sems.at[1]),
    )


def weigh(pieces, beams, p):
    wide = beams[p].astype(F32)
    return [(wide * pieces[p, c].astype(F32)).astype(BF16) for c in range(pieces.shape[1])]


def pack_kernel(count, me_ref, owner_ref, pieces_hbm, beam_hbm, *refs):
    outs, (pieces, beams, packed, in_sems, out_sems) = refs[: count - 1], refs[count - 1 :]
    _, piece_count, channels, strip, _ = pieces.shape
    planes = channels + 1
    me = me_ref[0]

    def fetch(k):
        here = (pieces.at[k - 1], beams.at[k - 1], in_sems.at[k - 1])
        return fetch_strip(pieces_hbm, beam_hbm, *here, me ^ k)

    order = range(count - 1, 0, -1)
    for k in order:
        for copy in fetch(k):
            copy.start()
    row = lax.broadcasted_iota(jnp.int32, (strip, LANES), 0)
    plane = jnp.zeros((strip, LANES), jnp.int32)
    for p in range(piece_count):
        plane = jnp.where(row == p, owner_ref[p], plane)
    plane = plane.astype(F32).astype(BF16)
    for k in order:
        for copy in fetch(k):
            copy.wait()
        for p in range(piece_count):
            for c, value in enumerate(weigh(pieces.at[k - 1], beams.at[k - 1], p)):
                packed[k - 1, p * planes + c] = value
            packed[k - 1, p * planes + channels] = beams[k - 1, p]
        packed[k - 1, piece_count * planes] = plane
        pltpu.make_async_copy(packed.at[k - 1], outs[k - 1], out_sems.at[k - 1]).start()
    for k in order:
        pltpu.make_async_copy(packed.at[k - 1], outs[k - 1], out_sems.at[k - 1]).wait()


def pack(me, destination, parts, beams):
    piece_count, channels, count, strip, _ = parts.shape
    out = jax.ShapeDtypeStruct((piece_count * (channels + 1) + 1, strip, LANES), BF16)
    far = pl.BlockSpec(memory_space=pl.ANY)
    return pl.pallas_call(
        functools.partial(pack_kernel, count),
        in_specs=[SMEM, SMEM, far, far],
        out_specs=[far] * (count - 1),
        out_shape=[out] * (count - 1),
        scratch_shapes=[
            pltpu.VMEM((count - 1, piece_count, channels, strip, LANES), BF16),
            pltpu.VMEM((count - 1, piece_count, strip, LANES), BF16),
            pltpu.VMEM((count - 1,) + out.shape, BF16),
            pltpu.SemaphoreType.DMA((count - 1, 2)),
            pltpu.SemaphoreType.DMA((count - 1,)),
        ],
        compiler_params=params(58),
        cost_estimate=cost(parts.size, 4 * parts.size),
        name="pack_pieces",
    )(me, destination, parts, beams)


def gather_kernel(me_ref, owner_ref, pieces_hbm, beam_hbm, total, cover, pieces, beams, sems):
    copies = fetch_strip(pieces_hbm, beam_hbm, pieces, beams, sems, me_ref[0])
    for copy in copies:
        copy.start()
    total[...] = jnp.zeros_like(total)
    cover[...] = jnp.full(cover.shape, REGULARIZER, F32)
    for copy in copies:
        copy.wait()
    for p in range(pieces.shape[0]):
        block = owner_ref[p]
        beam = beams[p].astype(F32)
        cover[block] += beam * beam
        for c, value in enumerate(weigh(pieces, beams, p)):
            total[block, c] += value.astype(F32)


def gather_own(me, destination, parts, beams):
    piece_count, channels, count, strip, _ = parts.shape
    blocks = count * COLB
    far = pl.BlockSpec(memory_space=pl.ANY)
    return pl.pallas_call(
        gather_kernel,
        in_specs=[SMEM, SMEM, far, far],
        out_specs=[VMEM] * 2,
        out_shape=[
            jax.ShapeDtypeStruct((blocks, channels, strip, LANES), F32),
            jax.ShapeDtypeStruct((blocks, strip, LANES), F32),
        ],
        scratch_shapes=[
            pltpu.VMEM((piece_count, channels, strip, LANES), BF16),
            pltpu.VMEM((piece_count, strip, LANES), BF16),
            pltpu.SemaphoreType.DMA((2,)),
        ],
        compiler_params=params(24),
        cost_estimate=cost(parts.size, 4 * parts.size),
        name="gather_own",
    )(me, destination, parts, beams)


def write_strips(count, me, scale, total, outs):
    _, channels, strip, _ = total.shape
    first = me == 0
    last = me == count - 1
    for k, out in enumerate(outs):
        tile = me ^ k
        other = jnp.where(last, tile - 1, tile + 1)
        valid = jnp.logical_or(
            jnp.logical_and(last, tile > 0), jnp.logical_and(first, tile < count - 1)
        )
        other = jnp.clip(other, 0, count - 1)
        for column in range(COLB):
            lanes = slice(column * LANES, (column + 1) * LANES)
            block = tile * COLB + column
            factor = scale[block]
            for c in range(channels):
                out[c, :, lanes] = (total[block, c] * factor).astype(BF16)
            if out.shape[0] == channels:
                continue
            block = other * COLB + column
            rows = []
            for c in range(channels):
                high = total[block, c, strip - RIM :] * scale[block, strip - RIM :]
                low = total[block, c, :RIM] * scale[block, :RIM]
                rows.append(jnp.where(valid, jnp.where(last, high, low), 0.0))
            rims = jnp.concatenate(rows, axis=0)
            for e in range(channels * RIM // strip):
                out[channels + e, :, lanes] = rims[e * strip : (e + 1) * strip].astype(BF16)


def combine_kernel(count, piece_count, me_ref, total_in, cover_in, *refs):
    parts, outs = refs[: count - 1], refs[count - 1 : 2 * count - 1]
    total, cover, rows, table, sem = refs[2 * count - 1 :]
    planes = (parts[0].shape[0] - 1) // piece_count
    channels = planes - 1
    for i, part in enumerate(parts):
        plane = part[part.shape[0] - 1].astype(F32)[:piece_count]
        rows[i * piece_count : (i + 1) * piece_count] = plane.astype(jnp.int32)
    copy = pltpu.make_async_copy(rows, table, sem)
    copy.start()
    total[...] = total_in[...]
    cover[...] = cover_in[...]
    copy.wait()
    for i, part in enumerate(parts):

        def add(p, _, i=i, part=part):
            block = table[i * piece_count + p, 0]
            beam = part[p * planes + channels].astype(F32)
            cover[block] += beam * beam
            total[block] += part[pl.ds(p * planes, channels)].astype(F32)
            return 0

        lax.fori_loop(0, piece_count, add, 0)
    cover[...] = 1.0 / cover[...]
    write_strips(count, me_ref[0], cover, total, outs)


def combine(me, total, cover, parts, piece_count):
    count = len(parts) + 1
    blocks, channels, strip, _ = total.shape
    rim_planes = channels * RIM // strip
    outs = [
        jax.ShapeDtypeStruct((channels + rim_planes * (k != count - 1), strip, COLB * LANES), BF16)
        for k in range(count)
    ]
    rows = len(parts) * piece_count
    return pl.pallas_call(
        functools.partial(combine_kernel, count, piece_count),
        in_specs=[SMEM] + [VMEM] * (2 + len(parts)),
        out_specs=[VMEM] * count,
        out_shape=outs,
        scratch_shapes=[
            pltpu.VMEM(total.shape, F32),
            pltpu.VMEM(cover.shape, F32),
            pltpu.VMEM((rows, LANES), jnp.int32),
            pltpu.SMEM((rows, LANES), jnp.int32),
            pltpu.SemaphoreType.DMA,
        ],
        compiler_params=params(20),
        cost_estimate=cost(1, 1),
        name="combine_strips",
    )(me, total, cover, *parts)


def edge_rows(me, strips, channels, c):
    count = len(strips) + 1
    strip, broad = strips[0].shape[1:]
    above = jnp.zeros((RIM, broad), F32)
    below = jnp.zeros((RIM, broad), F32)
    plane, row = divmod(c * RIM, strip)
    for k, part in enumerate(strips):
        rim = part[channels + plane].astype(F32)[row : row + RIM]
        source = me ^ k
        above = jnp.where(source == count - 1, rim, above)
        below = jnp.where(source == 0, rim, below)
    return [above, below]


def stack_rows(parts):
    if all(part.shape[0] % 16 == 0 for part in parts):
        return jnp.concatenate(parts, axis=0)
    return jnp.concatenate([part.astype(F32) for part in parts], axis=0).astype(BF16)


def tile_plane(me, strips, channels, c):
    edges = jnp.concatenate(edge_rows(me, strips[:-1], channels, c), axis=0).astype(BF16)
    return stack_rows([part[c] for part in strips] + [edges])


def join_kernel(me_ref, *refs):
    strips, (lower, upper) = refs[:-2], refs[-2:]
    channels = strips[-1].shape[0]
    for c in range(channels):
        plane = tile_plane(me_ref[0], strips, channels, c)
        if c < EDGE:
            lower[c] = plane
        if c >= channels - EDGE:
            upper[c - (channels - EDGE)] = plane


def join(me, strips):
    _, strip, broad = strips[0].shape
    out = jax.ShapeDtypeStruct((EDGE, len(strips) * strip + 2 * RIM, broad), BF16)
    return pl.pallas_call(
        join_kernel,
        in_specs=[SMEM] + [VMEM] * len(strips),
        out_specs=[VMEM] * 2,
        out_shape=[out] * 2,
        compiler_params=params(16),
        cost_estimate=cost(1, 1),
        name="join_strips",
    )(me, *strips)


def smooth_planes(planes, down, across, middle, out, base):
    tall = down.shape[0] // KERNELS
    broad = across.shape[2] * 2
    half = broad // 2
    at = len(planes)
    for i, plane in enumerate(planes):
        found = jnp.dot(down[...], plane(), preferred_element_type=F32).astype(BF16)
        for k in range(KERNELS):
            middle[k, i * tall : (i + 1) * tall] = found[k * tall : (k + 1) * tall]
    chunks = -(-at // 4)
    sizes = [at // chunks + (i < at % chunks) for i in range(chunks)]
    for k in range(KERNELS):
        start = 0
        for size in sizes:
            rows = slice(start * tall, (start + size) * tall)
            quarter = half // 2
            left = jnp.dot(middle[k, rows, :half], across[k, 0], preferred_element_type=F32)
            right = jnp.dot(middle[k, rows, half:], across[k, 1], preferred_element_type=F32)
            seam = jnp.dot(
                middle[k, rows, quarter : quarter + half], across[k, 2], preferred_element_type=F32
            )
            parts = [
                left[:, :quarter],
                left[:, quarter:] + seam[:, :quarter],
                right[:, :quarter] + seam[:, quarter:],
                right[:, quarter:],
            ]
            for i, part in enumerate(parts):
                lanes = slice(i * quarter, (i + 1) * quarter)
                value = part.astype(BF16).reshape(size, tall, quarter)
                out[k, base + start : base + start + size, :, lanes] = value
            start += size


def smooth_kernel(count, me_ref, down, across, *refs):
    strips, (out, middle) = refs[:count], refs[count:]
    me = me_ref[0]
    channels = out.shape[1]

    planes = [functools.partial(tile_plane, me, strips, channels, c) for c in range(channels)]
    smooth_planes(planes, down.at[me], across, middle, out, 0)


def smooth(me, strips, down, across):
    channels = strips[-1].shape[0]
    broad = strips[0].shape[2]
    tall = down.shape[1] // KERNELS
    out = jax.ShapeDtypeStruct((KERNELS, channels, tall, broad), BF16)
    return pl.pallas_call(
        functools.partial(smooth_kernel, len(strips)),
        in_specs=[SMEM] + [VMEM] * (2 + len(strips)),
        out_specs=VMEM,
        out_shape=out,
        scratch_shapes=[pltpu.VMEM((KERNELS, channels * tall, broad), BF16)],
        compiler_params=params(16),
        cost_estimate=cost(2 * out.size * (broad + 256), 4 * out.size),
        name="smooth_own",
    )(me, down, across, *strips)


def boxcars(load, channels):
    x, two, four, eight, one, three = {}, {}, {}, {}, {}, {}
    for i in range(channels + 2 * EDGE):
        x[i] = load(i)
        if i >= 1:
            two[i - 1] = x[i - 1] + x[i]
        if i >= 3:
            four[i - 3] = two[i - 3] + two[i - 1]
        if i >= 7:
            eight[i - 7] = four[i - 7] + four[i - 3]
        if i >= 2:
            one[i - 1] = two[i - 2] + x[i]
        if i >= 6:
            three[i - 3] = four[i - 6] + one[i - 1]
        ready = [(0, i, x), (1, i - 1, one), (2, i - 3, three)]
        for w, center, table in ready:
            if EDGE <= center < EDGE + channels:
                yield w, center - EDGE, table[center]
        if i >= 2 * EDGE:
            yield 3, i - 2 * EDGE, eight[i - 14] + three[i - 3]


def layer_order(channels):
    order = [(1, c) for c in range(EDGE)]
    order += [(0, c) for c in range(channels)]
    order += [(1, c) for c in range(EDGE, 2 * EDGE)]
    return order


def power_kernel(me_ref, down, across, own, low, high, halo, power, middle, sums):
    channels, tall, broad = own.shape[1:]
    for side, base in ((low, 0), (high, EDGE)):
        planes = [functools.partial(side.__getitem__, c) for c in range(EDGE)]
        smooth_planes(planes, down.at[me_ref[0]], across, middle, halo, base)
    layers = (own, halo)
    order = layer_order(channels)
    sums[...] = jnp.zeros_like(sums)
    lane_groups = broad // LANES

    def add(step, _):
        rows = pl.ds(pl.multiple_of(step // lane_groups * 16, 16), 16)
        lanes = pl.ds(pl.multiple_of(step % lane_groups * LANES, LANES), LANES)
        for k in range(KERNELS):

            def load(i, k=k):
                array, plane = order[i]
                return layers[array][k, plane, rows, lanes].astype(F32)

            for w, c, value in boxcars(load, channels):
                square = value * value
                sums[(k * WIDTHS + w) * channels + c] += square[:8] + square[8:]
        return 0

    lax.fori_loop(0, tall // 16 * lane_groups, add, 0)
    total = jnp.sum(jnp.sum(sums[...], axis=1), axis=1, keepdims=True)
    power[...] = jnp.broadcast_to(total, power.shape)


def smooth_power(me, own, sides, down, across):
    _, channels, tall, broad = own.shape
    pairs = KERNELS * WIDTHS * channels
    halo = jax.ShapeDtypeStruct((KERNELS, 2 * EDGE, tall, broad), BF16)
    return pl.pallas_call(
        power_kernel,
        in_specs=[SMEM] + [VMEM] * (3 + len(sides)),
        out_specs=[VMEM] * 2,
        out_shape=[halo, jax.ShapeDtypeStruct((pairs, LANES), F32)],
        scratch_shapes=[
            pltpu.VMEM((KERNELS, EDGE * tall, broad), BF16),
            pltpu.VMEM((pairs, 8, LANES), F32),
        ],
        compiler_params=params(24),
        cost_estimate=cost(2 * halo.size * (broad + 256), 8 * halo.size),
        name="smooth_power",
    )(me, down, across, own, *sides)


def score_kernel(count, cells, own, halo, clips, *refs):
    layers, powers = (own, halo), refs[:count]
    out, factor = refs[-2:]
    channels, step_rows, broad = out.shape
    order = layer_order(channels)

    @pl.when(pl.program_id(0) == 0)
    def _():
        total = powers[0][...]
        for item in powers[1:]:
            total = total + item[...]
        noise = jnp.sqrt(total / cells + EPSILON)
        for k in range(KERNELS):
            for w in range(WIDTHS):
                rows = slice((k * WIDTHS + w) * channels, (k * WIDTHS + w + 1) * channels)
                scale = 10.0 / (clips[k, w].astype(F32) * noise[rows])
                factor[rows] = jnp.broadcast_to(scale[:, None], (channels,) + factor.shape[1:])

    lane_groups = broad // LANES
    base = pl.program_id(0) * step_rows

    def score(step, _):
        start = pl.multiple_of(step // lane_groups * 16, 16)
        rows = pl.ds(pl.multiple_of(base + start, 16), 16)
        lanes = pl.ds(pl.multiple_of(step % lane_groups * LANES, LANES), LANES)
        best = [None] * channels
        for k in range(KERNELS):

            def load(i, k=k):
                array, plane = order[i]
                return layers[array][k, plane, rows, lanes].astype(F32).reshape(2, 8, LANES)

            for w, c, value in boxcars(load, channels):
                value = jnp.abs(value) * factor[(k * WIDTHS + w) * channels + c]
                best[c] = value if best[c] is None else jnp.maximum(best[c], value)
        for c in range(channels):
            out[c, pl.ds(start, 16), lanes] = best[c].reshape(16, LANES)
        return 0

    lax.fori_loop(0, step_rows // 16 * lane_groups, score, 0)


def score(own, halo, clips, powers, cells):
    _, channels, tall, broad = own.shape
    pairs = KERNELS * WIDTHS * channels
    step = 32
    return pl.pallas_call(
        functools.partial(score_kernel, len(powers), cells),
        grid=(tall // step,),
        in_specs=[VMEM, VMEM, SMEM] + [VMEM] * len(powers),
        out_specs=pl.BlockSpec((channels, step, broad), lambda i: (0, i, 0)),
        out_shape=jax.ShapeDtypeStruct((channels, tall, broad), F32),
        scratch_shapes=[pltpu.VMEM((pairs, 8, LANES), F32)],
        compiler_params=params(14),
        cost_estimate=cost(40 * KERNELS * channels * tall * broad, 8 * own.size),
        name="score_cells",
    )(own, halo, clips, *powers)


def shards(across_table, down_table, pieces, beam, destination, clip_tenths):
    count = lax.axis_size("sky")
    links = lax.axis_size("freq")
    piece_count, channels = pieces.shape[:2]
    me = lax.axis_index("sky").astype(jnp.int32).reshape(1)
    across = jnp.asarray(across_table)
    down = jnp.asarray(down_table)

    strip = LANES // count
    parts = pieces.reshape(piece_count, channels, count, strip, LANES)
    beams = beam.reshape(piece_count, count, strip, LANES)
    packed = pack(me, destination, parts, beams)
    arrived = [exchange(block, "sky", k) for k, block in enumerate(packed, 1)]
    total, cover = gather_own(me, destination, parts, beams)
    strips = combine(me, total, cover, arrived, piece_count)
    tiles = [strips[0]] + [exchange(strips[k], "sky", k) for k in range(1, count)]
    lower, upper = join(me, tiles)
    sides = [
        lax.ppermute(upper, "freq", [(i, i + 1) for i in range(links - 1)]),
        lax.ppermute(lower, "freq", [(i + 1, i) for i in range(links - 1)]),
    ]
    own = smooth(me, tiles, down, across)
    halo, power = smooth_power(me, own, sides, down, across)
    powers = [power] + [exchange(power, "sky", k) for k in range(1, count)]
    cells = float(count * ROWB * LANES * COLB * LANES)
    return score(own, halo, clip_tenths, powers, cells)


def solution(mesh):
    count = mesh.shape["sky"]
    body = functools.partial(
        shards, across_matrices(COLB * LANES), down_matrices(count, ROWB * LANES // count)
    )
    return jax.shard_map(
        body,
        mesh=mesh,
        in_specs=(P("sky", "freq", None, None), P("sky", None, None), P("sky"), P()),
        out_specs=P("freq", "sky", None),
        check_vma=False,
    )
```

```python
import functools

import jax
import jax.numpy as jnp
import ml_dtypes
import numpy as np
from jax import lax
from jax.experimental import pallas as pl
from jax.experimental.pallas import tpu as pltpu
from jax.sharding import PartitionSpec as P

ROWB = 1
COLB = 4
RIM = 8
EDGE = 7
KERNELS = 3
WIDTHS = 4

REGULARIZER = 0.05
EPSILON = 1e-06
KERNEL_FWHM = (3.0, 6.0, 9.0)
HALF_WIDTHS = (0, 1, 3, 7)

LANES = 128
MIB = 1 << 20
F32 = jnp.float32
BF16 = jnp.bfloat16
SMEM = pl.BlockSpec(memory_space=pltpu.SMEM)
VMEM = pl.BlockSpec(memory_space=pltpu.VMEM)


def params(mib):
    return pltpu.CompilerParams(vmem_limit_bytes=mib * MIB)


def cost(flops, moved):
    return pl.CostEstimate(flops=int(flops), bytes_accessed=int(moved), transcendentals=0)


def tap_table(distance):
    offsets = np.arange(-RIM, RIM + 1).astype(np.float32)
    near = np.abs(distance) <= RIM
    index = np.clip(distance + RIM, 0, 2 * RIM)
    found = []
    for fwhm in KERNEL_FWHM:
        sigma = np.float32(fwhm / 2.3548)
        taps = np.exp(-offsets * offsets / (np.float32(2.0) * sigma * sigma)).astype(ml_dtypes.bfloat16)
        found.append(np.where(near, taps[index], np.zeros((), ml_dtypes.bfloat16)))
    return np.stack(found)


def across_matrices(broad):
    half = broad // 2
    cells = np.arange(broad)
    table = tap_table(cells[:, None] - cells[None, :])
    middle = slice(half // 2, half // 2 + half)
    seam = (cells[middle, None] < half) != (cells[None, middle] < half)
    crossing = np.where(seam[None], table[:, middle, middle], np.zeros((), ml_dtypes.bfloat16))
    return np.stack([table[:, :half, :half], table[:, half:, half:], crossing], axis=1)


def down_matrices(count, strip):
    tall = count * strip
    found = []
    for me in range(count):
        rows = [(me ^ k) * strip + np.arange(strip) for k in range(count)]
        rows += [np.arange(-RIM, 0), np.arange(tall, tall + RIM)]
        rows = np.concatenate(rows)
        found.append(tap_table(rows[None, :] - np.arange(tall)[:, None]).reshape(KERNELS * tall, tall + 2 * RIM))
    return np.stack(found)


def exchange(block, axis, k):
    count = lax.axis_size(axis)
    return lax.ppermute(block, axis, [(i, i ^ k) for i in range(count)])


def fetch_strip(pieces_hbm, beam_hbm, pieces, beams, sems, target):
    return (
        pltpu.make_async_copy(beam_hbm.at[:, target], beams, sems.at[0]),
        pltpu.make_async_copy(pieces_hbm.at[:, :, target], pieces, sems.at[1]),
    )


def weigh(pieces, beams, p):
    wide = beams[p].astype(F32)
    return [(wide * pieces[p, c].astype(F32)).astype(BF16) for c in range(pieces.shape[1])]


def pack_kernel(count, me_ref, owner_ref, pieces_hbm, beam_hbm, *refs):
    outs, (pieces, beams, packed, in_sems, out_sems) = refs[: count - 1], refs[count - 1 :]
    _, piece_count, channels, strip, _ = pieces.shape
    planes = channels + 1
    me = me_ref[0]

    def fetch(k):
        here = (pieces.at[k - 1], beams.at[k - 1], in_sems.at[k - 1])
        return fetch_strip(pieces_hbm, beam_hbm, *here, me ^ k)

    order = range(count - 1, 0, -1)
    for k in order:
        for copy in fetch(k):
            copy.start()
    row = lax.broadcasted_iota(jnp.int32, (strip, LANES), 0)
    plane = jnp.zeros((strip, LANES), jnp.int32)
    for p in range(piece_count):
        plane = jnp.where(row == p, owner_ref[p], plane)
    plane = plane.astype(F32).astype(BF16)
    for k in order:
        for copy in fetch(k):
            copy.wait()
        for p in range(piece_count):
            for c, value in enumerate(weigh(pieces.at[k - 1], beams.at[k - 1], p)):
                packed[k - 1, p * planes + c] = value
            packed[k - 1, p * planes + channels] = beams[k - 1, p]
        packed[k - 1, piece_count * planes] = plane
        pltpu.make_async_copy(packed.at[k - 1], outs[k - 1], out_sems.at[k - 1]).start()
    for k in order:
        pltpu.make_async_copy(packed.at[k - 1], outs[k - 1], out_sems.at[k - 1]).wait()


def pack(me, destination, parts, beams):
    piece_count, channels, count, strip, _ = parts.shape
    out = jax.ShapeDtypeStruct((piece_count * (channels + 1) + 1, strip, LANES), BF16)
    far = pl.BlockSpec(memory_space=pl.ANY)
    return pl.pallas_call(
        functools.partial(pack_kernel, count),
        in_specs=[SMEM, SMEM, far, far],
        out_specs=[far] * (count - 1),
        out_shape=[out] * (count - 1),
        scratch_shapes=[
            pltpu.VMEM((count - 1, piece_count, channels, strip, LANES), BF16),
            pltpu.VMEM((count - 1, piece_count, strip, LANES), BF16),
            pltpu.VMEM((count - 1,) + out.shape, BF16),
            pltpu.SemaphoreType.DMA((count - 1, 2)),
            pltpu.SemaphoreType.DMA((count - 1,)),
        ],
        compiler_params=params(58),
        cost_estimate=cost(parts.size, 4 * parts.size),
        name="pack_pieces",
    )(me, destination, parts, beams)


def gather_kernel(me_ref, owner_ref, pieces_hbm, beam_hbm, total, cover, pieces, beams, sems):
    copies = fetch_strip(pieces_hbm, beam_hbm, pieces, beams, sems, me_ref[0])
    for copy in copies:
        copy.start()
    total[...] = jnp.zeros_like(total)
    cover[...] = jnp.full(cover.shape, REGULARIZER, F32)
    for copy in copies:
        copy.wait()
    for p in range(pieces.shape[0]):
        block = owner_ref[p]
        beam = beams[p].astype(F32)
        cover[block] += beam * beam
        for c, value in enumerate(weigh(pieces, beams, p)):
            total[block, c] += value.astype(F32)


def gather_own(me, destination, parts, beams):
    piece_count, channels, count, strip, _ = parts.shape
    blocks = count * COLB
    far = pl.BlockSpec(memory_space=pl.ANY)
    return pl.pallas_call(
        gather_kernel,
        in_specs=[SMEM, SMEM, far, far],
        out_specs=[VMEM] * 2,
        out_shape=[
            jax.ShapeDtypeStruct((blocks, channels, strip, LANES), F32),
            jax.ShapeDtypeStruct((blocks, strip, LANES), F32),
        ],
        scratch_shapes=[
            pltpu.VMEM((piece_count, channels, strip, LANES), BF16),
            pltpu.VMEM((piece_count, strip, LANES), BF16),
            pltpu.SemaphoreType.DMA((2,)),
        ],
        compiler_params=params(24),
        cost_estimate=cost(parts.size, 4 * parts.size),
        name="gather_own",
    )(me, destination, parts, beams)


def write_strips(count, me, scale, total, outs):
    _, channels, strip, _ = total.shape
    first = me == 0
    last = me == count - 1
    for k, out in enumerate(outs):
        tile = me ^ k
        other = jnp.where(last, tile - 1, tile + 1)
        valid = jnp.logical_or(
            jnp.logical_and(last, tile > 0), jnp.logical_and(first, tile < count - 1)
        )
        other = jnp.clip(other, 0, count - 1)
        for column in range(COLB):
            lanes = slice(column * LANES, (column + 1) * LANES)
            block = tile * COLB + column
            factor = scale[block]
            for c in range(channels):
                out[c, :, lanes] = (total[block, c] * factor).astype(BF16)
            if out.shape[0] == channels:
                continue
            block = other * COLB + column
            rows = []
            for c in range(channels):
                high = total[block, c, strip - RIM :] * scale[block, strip - RIM :]
                low = total[block, c, :RIM] * scale[block, :RIM]
                rows.append(jnp.where(valid, jnp.where(last, high, low), 0.0))
            rims = jnp.concatenate(rows, axis=0)
            for e in range(channels * RIM // strip):
                out[channels + e, :, lanes] = rims[e * strip : (e + 1) * strip].astype(BF16)


def combine_kernel(count, piece_count, me_ref, total_in, cover_in, *refs):
    parts, outs = refs[: count - 1], refs[count - 1 : 2 * count - 1]
    total, cover, rows, table, sem = refs[2 * count - 1 :]
    planes = (parts[0].shape[0] - 1) // piece_count
    channels = planes - 1
    for i, part in enumerate(parts):
        plane = part[part.shape[0] - 1].astype(F32)[:piece_count]
        rows[i * piece_count : (i + 1) * piece_count] = plane.astype(jnp.int32)
    copy = pltpu.make_async_copy(rows, table, sem)
    copy.start()
    total[...] = total_in[...]
    cover[...] = cover_in[...]
    copy.wait()
    for i, part in enumerate(parts):

        def add(p, _, i=i, part=part):
            block = table[i * piece_count + p, 0]
            beam = part[p * planes + channels].astype(F32)
            cover[block] += beam * beam
            total[block] += part[pl.ds(p * planes, channels)].astype(F32)
            return 0

        lax.fori_loop(0, piece_count, add, 0)
    cover[...] = 1.0 / cover[...]
    write_strips(count, me_ref[0], cover, total, outs)


def combine(me, total, cover, parts, piece_count):
    count = len(parts) + 1
    blocks, channels, strip, _ = total.shape
    rim_planes = channels * RIM // strip
    outs = [
        jax.ShapeDtypeStruct((channels + rim_planes * (k != count - 1), strip, COLB * LANES), BF16)
        for k in range(count)
    ]
    rows = len(parts) * piece_count
    return pl.pallas_call(
        functools.partial(combine_kernel, count, piece_count),
        in_specs=[SMEM] + [VMEM] * (2 + len(parts)),
        out_specs=[VMEM] * count,
        out_shape=outs,
        scratch_shapes=[
            pltpu.VMEM(total.shape, F32),
            pltpu.VMEM(cover.shape, F32),
            pltpu.VMEM((rows, LANES), jnp.int32),
            pltpu.SMEM((rows, LANES), jnp.int32),
            pltpu.SemaphoreType.DMA,
        ],
        compiler_params=params(20),
        cost_estimate=cost(1, 1),
        name="combine_strips",
    )(me, total, cover, *parts)


def edge_rows(me, strips, channels, c):
    count = len(strips) + 1
    strip, broad = strips[0].shape[1:]
    above = jnp.zeros((RIM, broad), F32)
    below = jnp.zeros((RIM, broad), F32)
    plane, row = divmod(c * RIM, strip)
    for k, part in enumerate(strips):
        rim = part[channels + plane].astype(F32)[row : row + RIM]
        source = me ^ k
        above = jnp.where(source == count - 1, rim, above)
        below = jnp.where(source == 0, rim, below)
    return [above, below]


def stack_rows(parts):
    if all(part.shape[0] % 16 == 0 for part in parts):
        return jnp.concatenate(parts, axis=0)
    return jnp.concatenate([part.astype(F32) for part in parts], axis=0).astype(BF16)


def tile_plane(me, strips, channels, c):
    edges = jnp.concatenate(edge_rows(me, strips[:-1], channels, c), axis=0).astype(BF16)
    return stack_rows([part[c] for part in strips] + [edges])


def join_kernel(me_ref, odd_ref, *refs):
    strips, (outer, inner) = refs[:-2], refs[-2:]
    channels = strips[-1].shape[0]
    odd = odd_ref[0]
    last = channels - EDGE
    starts = ((outer, odd * last), (inner, (1 - odd) * last))
    for c in range(channels):
        plane = tile_plane(me_ref[0], strips, channels, c)
        for out, start in starts:
            at = c - start

            @pl.when(jnp.logical_and(at >= 0, at < EDGE))
            def _(out=out, at=at, plane=plane):
                out[at] = plane


def join(me, odd, strips):
    _, strip, broad = strips[0].shape
    out = jax.ShapeDtypeStruct((EDGE, len(strips) * strip + 2 * RIM, broad), BF16)
    return pl.pallas_call(
        join_kernel,
        in_specs=[SMEM, SMEM] + [VMEM] * len(strips),
        out_specs=[VMEM] * 2,
        out_shape=[out] * 2,
        compiler_params=params(16),
        cost_estimate=cost(1, 1),
        name="join_strips",
    )(me, odd, *strips)


def smooth_planes(planes, down, across, middle, out, base):
    tall = down.shape[0] // KERNELS
    broad = across.shape[2] * 2
    half = broad // 2
    at = len(planes)
    for i, plane in enumerate(planes):
        found = jnp.dot(down[...], plane(), preferred_element_type=F32).astype(BF16)
        for k in range(KERNELS):
            middle[k, i * tall : (i + 1) * tall] = found[k * tall : (k + 1) * tall]
    chunks = -(-at // 4)
    sizes = [at // chunks + (i < at % chunks) for i in range(chunks)]
    for k in range(KERNELS):
        start = 0
        for size in sizes:
            rows = slice(start * tall, (start + size) * tall)
            quarter = half // 2
            left = jnp.dot(middle[k, rows, :half], across[k, 0], preferred_element_type=F32)
            right = jnp.dot(middle[k, rows, half:], across[k, 1], preferred_element_type=F32)
            seam = jnp.dot(
                middle[k, rows, quarter : quarter + half], across[k, 2], preferred_element_type=F32
            )
            parts = [
                left[:, :quarter],
                left[:, quarter:] + seam[:, :quarter],
                right[:, :quarter] + seam[:, quarter:],
                right[:, quarter:],
            ]
            for i, part in enumerate(parts):
                lanes = slice(i * quarter, (i + 1) * quarter)
                value = part.astype(BF16).reshape(size, tall, quarter)
                out[k, pl.ds(base + start, size), :, lanes] = value
            start += size


def smooth_kernel(count, me_ref, down, across, *refs):
    strips, (out, middle) = refs[:count], refs[count:]
    me = me_ref[0]
    channels = out.shape[1]

    planes = [functools.partial(tile_plane, me, strips, channels, c) for c in range(channels)]
    smooth_planes(planes, down.at[me], across, middle, out, 0)


def smooth(me, strips, down, across):
    channels = strips[-1].shape[0]
    broad = strips[0].shape[2]
    tall = down.shape[1] // KERNELS
    out = jax.ShapeDtypeStruct((KERNELS, channels, tall, broad), BF16)
    return pl.pallas_call(
        functools.partial(smooth_kernel, len(strips)),
        in_specs=[SMEM] + [VMEM] * (2 + len(strips)),
        out_specs=VMEM,
        out_shape=out,
        scratch_shapes=[pltpu.VMEM((KERNELS, channels * tall, broad), BF16)],
        compiler_params=params(16),
        cost_estimate=cost(2 * out.size * (broad + 256), 4 * out.size),
        name="smooth_own",
    )(me, down, across, *strips)


def boxcars(load, channels):
    x, two, four, eight, one, three = {}, {}, {}, {}, {}, {}
    for i in range(channels + 2 * EDGE):
        x[i] = load(i)
        if i >= 1:
            two[i - 1] = x[i - 1] + x[i]
        if i >= 3:
            four[i - 3] = two[i - 3] + two[i - 1]
        if i >= 7:
            eight[i - 7] = four[i - 7] + four[i - 3]
        if i >= 2:
            one[i - 1] = two[i - 2] + x[i]
        if i >= 6:
            three[i - 3] = four[i - 6] + one[i - 1]
        ready = [(0, i, x), (1, i - 1, one), (2, i - 3, three)]
        for w, center, table in ready:
            if EDGE <= center < EDGE + channels:
                yield w, center - EDGE, table[center]
        if i >= 2 * EDGE:
            yield 3, i - 2 * EDGE, eight[i - 14] + three[i - 3]


def layer_order(channels):
    order = [(1, c) for c in range(EDGE)]
    order += [(0, c) for c in range(channels)]
    order += [(1, c) for c in range(EDGE, 2 * EDGE)]
    return order


def power_kernel(me_ref, odd_ref, down, across, own, outer, inner, halo, power, middle, sums):
    channels, tall, broad = own.shape[1:]
    odd = odd_ref[0]
    for side, base in ((inner, (1 - odd) * EDGE), (outer, odd * EDGE)):
        planes = [functools.partial(side.__getitem__, c) for c in range(EDGE)]
        smooth_planes(planes, down.at[me_ref[0]], across, middle, halo, base)
    layers = (own, halo)
    order = layer_order(channels)
    sums[...] = jnp.zeros_like(sums)
    lane_groups = broad // LANES

    def add(step, _):
        rows = pl.ds(pl.multiple_of(step // lane_groups * 16, 16), 16)
        lanes = pl.ds(pl.multiple_of(step % lane_groups * LANES, LANES), LANES)
        for k in range(KERNELS):

            def load(i, k=k):
                array, plane = order[i]
                return layers[array][k, plane, rows, lanes].astype(F32)

            for w, c, value in boxcars(load, channels):
                square = value * value
                sums[(k * WIDTHS + w) * channels + c] += square[:8] + square[8:]
        return 0

    lax.fori_loop(0, tall // 16 * lane_groups, add, 0)
    total = jnp.sum(jnp.sum(sums[...], axis=1), axis=1, keepdims=True)
    power[...] = jnp.broadcast_to(total, power.shape)


def smooth_power(me, odd, own, sides, down, across):
    _, channels, tall, broad = own.shape
    pairs = KERNELS * WIDTHS * channels
    halo = jax.ShapeDtypeStruct((KERNELS, 2 * EDGE, tall, broad), BF16)
    return pl.pallas_call(
        power_kernel,
        in_specs=[SMEM, SMEM] + [VMEM] * (3 + len(sides)),
        out_specs=[VMEM] * 2,
        out_shape=[halo, jax.ShapeDtypeStruct((pairs, LANES), F32)],
        scratch_shapes=[
            pltpu.VMEM((KERNELS, EDGE * tall, broad), BF16),
            pltpu.VMEM((pairs, 8, LANES), F32),
        ],
        compiler_params=params(24),
        cost_estimate=cost(2 * halo.size * (broad + 256), 8 * halo.size),
        name="smooth_power",
    )(me, odd, down, across, own, *sides)


def score_kernel(count, cells, own, halo, clips, *refs):
    layers, powers = (own, halo), refs[:count]
    out, factor = refs[-2:]
    channels, step_rows, broad = out.shape
    order = layer_order(channels)

    @pl.when(pl.program_id(0) == 0)
    def _():
        total = powers[0][...]
        for item in powers[1:]:
            total = total + item[...]
        noise = jnp.sqrt(total / cells + EPSILON)
        for k in range(KERNELS):
            for w in range(WIDTHS):
                rows = slice((k * WIDTHS + w) * channels, (k * WIDTHS + w + 1) * channels)
                scale = 10.0 / (clips[k, w].astype(F32) * noise[rows])
                factor[rows] = jnp.broadcast_to(scale[:, None], (channels,) + factor.shape[1:])

    lane_groups = broad // LANES
    base = pl.program_id(0) * step_rows

    def score(step, _):
        start = pl.multiple_of(step // lane_groups * 16, 16)
        rows = pl.ds(pl.multiple_of(base + start, 16), 16)
        lanes = pl.ds(pl.multiple_of(step % lane_groups * LANES, LANES), LANES)
        best = [None] * channels
        for k in range(KERNELS):

            def load(i, k=k):
                array, plane = order[i]
                return layers[array][k, plane, rows, lanes].astype(F32).reshape(2, 8, LANES)

            for w, c, value in boxcars(load, channels):
                value = jnp.abs(value) * factor[(k * WIDTHS + w) * channels + c]
                best[c] = value if best[c] is None else jnp.maximum(best[c], value)
        for c in range(channels):
            out[c, pl.ds(start, 16), lanes] = best[c].reshape(16, LANES)
        return 0

    lax.fori_loop(0, step_rows // 16 * lane_groups, score, 0)


def score(own, halo, clips, powers, cells):
    _, channels, tall, broad = own.shape
    pairs = KERNELS * WIDTHS * channels
    step = 32
    return pl.pallas_call(
        functools.partial(score_kernel, len(powers), cells),
        grid=(tall // step,),
        in_specs=[VMEM, VMEM, SMEM] + [VMEM] * len(powers),
        out_specs=pl.BlockSpec((channels, step, broad), lambda i: (0, i, 0)),
        out_shape=jax.ShapeDtypeStruct((channels, tall, broad), F32),
        scratch_shapes=[pltpu.VMEM((pairs, 8, LANES), F32)],
        compiler_params=params(14),
        cost_estimate=cost(40 * KERNELS * channels * tall * broad, 8 * own.size),
        name="score_cells",
    )(own, halo, clips, *powers)


def shards(across_table, down_table, pieces, beam, destination, clip_tenths):
    count = lax.axis_size("sky")
    links = lax.axis_size("freq")
    piece_count, channels = pieces.shape[:2]
    me = lax.axis_index("sky").astype(jnp.int32).reshape(1)
    across = jnp.asarray(across_table)
    down = jnp.asarray(down_table)

    strip = LANES // count
    parts = pieces.reshape(piece_count, channels, count, strip, LANES)
    beams = beam.reshape(piece_count, count, strip, LANES)
    packed = pack(me, destination, parts, beams)
    arrived = [exchange(block, "sky", k) for k, block in enumerate(packed, 1)]
    total, cover = gather_own(me, destination, parts, beams)
    strips = combine(me, total, cover, arrived, piece_count)
    tiles = [strips[0]] + [exchange(strips[k], "sky", k) for k in range(1, count)]
    odd = lax.rem(lax.axis_index("freq").astype(jnp.int32), 2).reshape(1)
    outer, inner = join(me, odd, tiles)
    outer_pairs = [(i, i + 1) for i in range(1, links - 1, 2)]
    inner_pairs = [(i, i + 1) for i in range(0, links - 1, 2)]
    sides = [
        lax.ppermute(block, "freq", pairs + [(target, source) for source, target in pairs])
        for block, pairs in ((outer, outer_pairs), (inner, inner_pairs))
    ]
    own = smooth(me, tiles, down, across)
    halo, power = smooth_power(me, odd, own, sides, down, across)
    powers = [power] + [exchange(power, "sky", k) for k in range(1, count)]
    cells = float(count * ROWB * LANES * COLB * LANES)
    return score(own, halo, clip_tenths, powers, cells)


def solution(mesh):
    count = mesh.shape["sky"]
    body = functools.partial(
        shards, across_matrices(COLB * LANES), down_matrices(count, ROWB * LANES // count)
    )
    return jax.shard_map(
        body,
        mesh=mesh,
        in_specs=(P("sky", "freq", None, None), P("sky", None, None), P("sky"), P()),
        out_specs=P("freq", "sky", None),
        check_vma=False,
    )
```

```python
import functools

import jax
import jax.numpy as jnp
import ml_dtypes
import numpy as np
from jax import lax
from jax.experimental import pallas as pl
from jax.experimental.pallas import tpu as pltpu
from jax.sharding import PartitionSpec as P

ROWB = 1
COLB = 4
RIM = 8
EDGE = 7
KERNELS = 3
WIDTHS = 4

REGULARIZER = 0.05
EPSILON = 1e-06
KERNEL_FWHM = (3.0, 6.0, 9.0)
HALF_WIDTHS = (0, 1, 3, 7)

LANES = 128
MIB = 1 << 20
F32 = jnp.float32
BF16 = jnp.bfloat16
SMEM = pl.BlockSpec(memory_space=pltpu.SMEM)
VMEM = pl.BlockSpec(memory_space=pltpu.VMEM)


def params(mib):
    return pltpu.CompilerParams(vmem_limit_bytes=mib * MIB)


def cost(flops, moved):
    return pl.CostEstimate(flops=int(flops), bytes_accessed=int(moved), transcendentals=0)


def tap_table(distance):
    offsets = np.arange(-RIM, RIM + 1).astype(np.float32)
    near = np.abs(distance) <= RIM
    index = np.clip(distance + RIM, 0, 2 * RIM)
    found = []
    for fwhm in KERNEL_FWHM:
        sigma = np.float32(fwhm / 2.3548)
        taps = np.exp(-offsets * offsets / (np.float32(2.0) * sigma * sigma)).astype(ml_dtypes.bfloat16)
        found.append(np.where(near, taps[index], np.zeros((), ml_dtypes.bfloat16)))
    return np.stack(found)


def across_matrices(broad):
    half = broad // 2
    cells = np.arange(broad)
    table = tap_table(cells[:, None] - cells[None, :])
    middle = slice(half // 2, half // 2 + half)
    seam = (cells[middle, None] < half) != (cells[None, middle] < half)
    crossing = np.where(seam[None], table[:, middle, middle], np.zeros((), ml_dtypes.bfloat16))
    return np.stack([table[:, :half, :half], table[:, half:, half:], crossing], axis=1)


def down_matrices(count, strip):
    tall = count * strip
    found = []
    for me in range(count):
        rows = [(me ^ k) * strip + np.arange(strip) for k in range(count)]
        rows += [np.arange(-RIM, 0), np.arange(tall, tall + RIM)]
        rows = np.concatenate(rows)
        found.append(tap_table(rows[None, :] - np.arange(tall)[:, None]).reshape(KERNELS * tall, tall + 2 * RIM))
    return np.stack(found)


def exchange(block, axis, k):
    count = lax.axis_size(axis)
    return lax.ppermute(block, axis, [(i, i ^ k) for i in range(count)])


def fetch_strip(pieces_hbm, beam_hbm, pieces, beams, sems, target):
    return (
        pltpu.make_async_copy(beam_hbm.at[:, target], beams, sems.at[0]),
        pltpu.make_async_copy(pieces_hbm.at[:, :, target], pieces, sems.at[1]),
    )


def weigh(pieces, beams, p):
    wide = beams[p].astype(F32)
    return [(wide * pieces[p, c].astype(F32)).astype(BF16) for c in range(pieces.shape[1])]


def pack_kernel(offsets, me_ref, owner_ref, pieces_hbm, beam_hbm, *refs):
    parts = len(offsets)
    outs, (pieces, beams, packed, in_sems, out_sems) = refs[:parts], refs[parts:]
    _, piece_count, channels, strip, _ = pieces.shape
    planes = channels + 1
    me = me_ref[0]

    def fetch(k):
        here = (pieces.at[k - 1], beams.at[k - 1], in_sems.at[k - 1])
        return fetch_strip(pieces_hbm, beam_hbm, *here, me ^ offsets[k - 1])

    order = range(parts, 0, -1)
    for k in order:
        for copy in fetch(k):
            copy.start()
    row = lax.broadcasted_iota(jnp.int32, (strip, LANES), 0)
    plane = jnp.zeros((strip, LANES), jnp.int32)
    for p in range(piece_count):
        plane = jnp.where(row == p, owner_ref[p], plane)
    plane = plane.astype(F32).astype(BF16)
    for k in order:
        for copy in fetch(k):
            copy.wait()
        for p in range(piece_count):
            for c, value in enumerate(weigh(pieces.at[k - 1], beams.at[k - 1], p)):
                packed[k - 1, p * planes + c] = value
            packed[k - 1, p * planes + channels] = beams[k - 1, p]
        packed[k - 1, piece_count * planes] = plane
        pltpu.make_async_copy(packed.at[k - 1], outs[k - 1], out_sems.at[k - 1]).start()
    for k in order:
        pltpu.make_async_copy(packed.at[k - 1], outs[k - 1], out_sems.at[k - 1]).wait()


def pack(me, destination, parts, beams, offsets):
    piece_count, channels, _, strip, _ = parts.shape
    count = len(offsets) + 1
    out = jax.ShapeDtypeStruct((piece_count * (channels + 1) + 1, strip, LANES), BF16)
    far = pl.BlockSpec(memory_space=pl.ANY)
    return pl.pallas_call(
        functools.partial(pack_kernel, offsets),
        in_specs=[SMEM, SMEM, far, far],
        out_specs=[far] * (count - 1),
        out_shape=[out] * (count - 1),
        scratch_shapes=[
            pltpu.VMEM((count - 1, piece_count, channels, strip, LANES), BF16),
            pltpu.VMEM((count - 1, piece_count, strip, LANES), BF16),
            pltpu.VMEM((count - 1,) + out.shape, BF16),
            pltpu.SemaphoreType.DMA((count - 1, 2)),
            pltpu.SemaphoreType.DMA((count - 1,)),
        ],
        compiler_params=params(58),
        cost_estimate=cost(parts.size, 4 * parts.size),
        name="pack_pieces",
    )(me, destination, parts, beams)


def gather_kernel(me_ref, owner_ref, pieces_hbm, beam_hbm, total, cover, pieces, beams, sems):
    copies = fetch_strip(pieces_hbm, beam_hbm, pieces, beams, sems, me_ref[0])
    for copy in copies:
        copy.start()
    total[...] = jnp.zeros_like(total)
    cover[...] = jnp.full(cover.shape, REGULARIZER, F32)
    for copy in copies:
        copy.wait()
    for p in range(pieces.shape[0]):
        block = owner_ref[p]
        beam = beams[p].astype(F32)
        cover[block] += beam * beam
        for c, value in enumerate(weigh(pieces, beams, p)):
            total[block, c] += value.astype(F32)


def gather_own(me, destination, parts, beams):
    piece_count, channels, count, strip, _ = parts.shape
    blocks = count * COLB
    far = pl.BlockSpec(memory_space=pl.ANY)
    return pl.pallas_call(
        gather_kernel,
        in_specs=[SMEM, SMEM, far, far],
        out_specs=[VMEM] * 2,
        out_shape=[
            jax.ShapeDtypeStruct((blocks, channels, strip, LANES), F32),
            jax.ShapeDtypeStruct((blocks, strip, LANES), F32),
        ],
        scratch_shapes=[
            pltpu.VMEM((piece_count, channels, strip, LANES), BF16),
            pltpu.VMEM((piece_count, strip, LANES), BF16),
            pltpu.SemaphoreType.DMA((2,)),
        ],
        compiler_params=params(24),
        cost_estimate=cost(parts.size, 4 * parts.size),
        name="gather_own",
    )(me, destination, parts, beams)


def write_strips(count, me, scale, total, outs):
    _, channels, strip, _ = total.shape
    first = me == 0
    last = me == count - 1
    for k, out in enumerate(outs):
        tile = me ^ k
        other = jnp.where(last, tile - 1, tile + 1)
        valid = jnp.logical_or(
            jnp.logical_and(last, tile > 0), jnp.logical_and(first, tile < count - 1)
        )
        other = jnp.clip(other, 0, count - 1)
        for column in range(COLB):
            lanes = slice(column * LANES, (column + 1) * LANES)
            block = tile * COLB + column
            factor = scale[block]
            for c in range(channels):
                out[c, :, lanes] = (total[block, c] * factor).astype(BF16)
            if out.shape[0] == channels:
                continue
            block = other * COLB + column
            rows = []
            for c in range(channels):
                high = total[block, c, strip - RIM :] * scale[block, strip - RIM :]
                low = total[block, c, :RIM] * scale[block, :RIM]
                rows.append(jnp.where(valid, jnp.where(last, high, low), 0.0))
            rims = jnp.concatenate(rows, axis=0)
            for e in range(channels * RIM // strip):
                out[channels + e, :, lanes] = rims[e * strip : (e + 1) * strip].astype(BF16)


def combine_kernel(count, piece_count, me_ref, total_in, cover_in, *refs):
    parts, outs = refs[: count - 1], refs[count - 1 : 2 * count - 1]
    total, cover, rows, table, sem = refs[2 * count - 1 :]
    planes = (parts[0].shape[0] - 1) // piece_count
    channels = planes - 1
    for i, part in enumerate(parts):
        plane = part[part.shape[0] - 1].astype(F32)[:piece_count]
        rows[i * piece_count : (i + 1) * piece_count] = plane.astype(jnp.int32)
    copy = pltpu.make_async_copy(rows, table, sem)
    copy.start()
    total[...] = total_in[...]
    cover[...] = cover_in[...]
    copy.wait()
    for i, part in enumerate(parts):

        def add(p, _, i=i, part=part):
            block = table[i * piece_count + p, 0]
            beam = part[p * planes + channels].astype(F32)
            cover[block] += beam * beam
            total[block] += part[pl.ds(p * planes, channels)].astype(F32)
            return 0

        lax.fori_loop(0, piece_count, add, 0)
    cover[...] = 1.0 / cover[...]
    write_strips(count, me_ref[0], cover, total, outs)


def combine(me, total, cover, parts, piece_count):
    count = len(parts) + 1
    blocks, channels, strip, _ = total.shape
    rim_planes = channels * RIM // strip
    outs = [
        jax.ShapeDtypeStruct((channels + rim_planes * (k != count - 1), strip, COLB * LANES), BF16)
        for k in range(count)
    ]
    rows = len(parts) * piece_count
    return pl.pallas_call(
        functools.partial(combine_kernel, count, piece_count),
        in_specs=[SMEM] + [VMEM] * (2 + len(parts)),
        out_specs=[VMEM] * count,
        out_shape=outs,
        scratch_shapes=[
            pltpu.VMEM(total.shape, F32),
            pltpu.VMEM(cover.shape, F32),
            pltpu.VMEM((rows, LANES), jnp.int32),
            pltpu.SMEM((rows, LANES), jnp.int32),
            pltpu.SemaphoreType.DMA,
        ],
        compiler_params=params(20),
        cost_estimate=cost(1, 1),
        name="combine_strips",
    )(me, total, cover, *parts)


def edge_rows(me, strips, channels, c):
    count = len(strips) + 1
    strip, broad = strips[0].shape[1:]
    above = jnp.zeros((RIM, broad), F32)
    below = jnp.zeros((RIM, broad), F32)
    plane, row = divmod(c * RIM, strip)
    for k, part in enumerate(strips):
        rim = part[channels + plane].astype(F32)[row : row + RIM]
        source = me ^ k
        above = jnp.where(source == count - 1, rim, above)
        below = jnp.where(source == 0, rim, below)
    return [above, below]


def stack_rows(parts):
    if all(part.shape[0] % 16 == 0 for part in parts):
        return jnp.concatenate(parts, axis=0)
    return jnp.concatenate([part.astype(F32) for part in parts], axis=0).astype(BF16)


def tile_plane(me, strips, channels, c):
    edges = jnp.concatenate(edge_rows(me, strips[:-1], channels, c), axis=0).astype(BF16)
    return stack_rows([part[c] for part in strips] + [edges])


def join_kernel(me_ref, odd_ref, *refs):
    strips, (outer, inner) = refs[:-2], refs[-2:]
    channels = strips[-1].shape[0]
    odd = odd_ref[0]
    last = channels - EDGE
    starts = ((outer, odd * last), (inner, (1 - odd) * last))
    for c in range(channels):
        plane = tile_plane(me_ref[0], strips, channels, c)
        for out, start in starts:
            at = c - start

            @pl.when(jnp.logical_and(at >= 0, at < EDGE))
            def _(out=out, at=at, plane=plane):
                out[at] = plane


def join(me, odd, strips):
    _, strip, broad = strips[0].shape
    out = jax.ShapeDtypeStruct((EDGE, len(strips) * strip + 2 * RIM, broad), BF16)
    return pl.pallas_call(
        join_kernel,
        in_specs=[SMEM, SMEM] + [VMEM] * len(strips),
        out_specs=[VMEM] * 2,
        out_shape=[out] * 2,
        compiler_params=params(16),
        cost_estimate=cost(1, 1),
        name="join_strips",
    )(me, odd, *strips)


def smooth_planes(planes, down, across, middle, out, base):
    tall = down.shape[0] // KERNELS
    broad = across.shape[2] * 2
    half = broad // 2
    at = len(planes)
    for i, plane in enumerate(planes):
        found = jnp.dot(down[...], plane(), preferred_element_type=F32).astype(BF16)
        for k in range(KERNELS):
            middle[k, i * tall : (i + 1) * tall] = found[k * tall : (k + 1) * tall]
    chunks = -(-at // 4)
    sizes = [at // chunks + (i < at % chunks) for i in range(chunks)]
    for k in range(KERNELS):
        start = 0
        for size in sizes:
            rows = slice(start * tall, (start + size) * tall)
            quarter = half // 2
            left = jnp.dot(middle[k, rows, :half], across[k, 0], preferred_element_type=F32)
            right = jnp.dot(middle[k, rows, half:], across[k, 1], preferred_element_type=F32)
            seam = jnp.dot(
                middle[k, rows, quarter : quarter + half], across[k, 2], preferred_element_type=F32
            )
            parts = [
                left[:, :quarter],
                left[:, quarter:] + seam[:, :quarter],
                right[:, :quarter] + seam[:, quarter:],
                right[:, quarter:],
            ]
            for i, part in enumerate(parts):
                lanes = slice(i * quarter, (i + 1) * quarter)
                value = part.astype(BF16).reshape(size, tall, quarter)
                out[k, pl.ds(base + start, size), :, lanes] = value
            start += size


def smooth_kernel(count, me_ref, down, across, *refs):
    strips, (out, middle) = refs[:count], refs[count:]
    me = me_ref[0]
    channels = out.shape[1]

    planes = [functools.partial(tile_plane, me, strips, channels, c) for c in range(channels)]
    smooth_planes(planes, down.at[me], across, middle, out, 0)


def smooth(me, strips, down, across):
    channels = strips[-1].shape[0]
    broad = strips[0].shape[2]
    tall = down.shape[1] // KERNELS
    out = jax.ShapeDtypeStruct((KERNELS, channels, tall, broad), BF16)
    return pl.pallas_call(
        functools.partial(smooth_kernel, len(strips)),
        in_specs=[SMEM] + [VMEM] * (2 + len(strips)),
        out_specs=VMEM,
        out_shape=out,
        scratch_shapes=[pltpu.VMEM((KERNELS, channels * tall, broad), BF16)],
        compiler_params=params(16),
        cost_estimate=cost(2 * out.size * (broad + 256), 4 * out.size),
        name="smooth_own",
    )(me, down, across, *strips)


def boxcars(load, channels):
    x, two, four, eight, one, three = {}, {}, {}, {}, {}, {}
    for i in range(channels + 2 * EDGE):
        x[i] = load(i)
        if i >= 1:
            two[i - 1] = x[i - 1] + x[i]
        if i >= 3:
            four[i - 3] = two[i - 3] + two[i - 1]
        if i >= 7:
            eight[i - 7] = four[i - 7] + four[i - 3]
        if i >= 2:
            one[i - 1] = two[i - 2] + x[i]
        if i >= 6:
            three[i - 3] = four[i - 6] + one[i - 1]
        ready = [(0, i, x), (1, i - 1, one), (2, i - 3, three)]
        for w, center, table in ready:
            if EDGE <= center < EDGE + channels:
                yield w, center - EDGE, table[center]
        if i >= 2 * EDGE:
            yield 3, i - 2 * EDGE, eight[i - 14] + three[i - 3]


def layer_order(channels):
    order = [(1, c) for c in range(EDGE)]
    order += [(0, c) for c in range(channels)]
    order += [(1, c) for c in range(EDGE, 2 * EDGE)]
    return order


def power_kernel(me_ref, odd_ref, down, across, own, outer, inner, halo, power, middle, sums):
    channels, tall, broad = own.shape[1:]
    odd = odd_ref[0]
    for side, base in ((inner, (1 - odd) * EDGE), (outer, odd * EDGE)):
        planes = [functools.partial(side.__getitem__, c) for c in range(EDGE)]
        smooth_planes(planes, down.at[me_ref[0]], across, middle, halo, base)
    layers = (own, halo)
    order = layer_order(channels)
    sums[...] = jnp.zeros_like(sums)
    lane_groups = broad // LANES

    def add(step, _):
        rows = pl.ds(pl.multiple_of(step // lane_groups * 16, 16), 16)
        lanes = pl.ds(pl.multiple_of(step % lane_groups * LANES, LANES), LANES)
        for k in range(KERNELS):

            def load(i, k=k):
                array, plane = order[i]
                return layers[array][k, plane, rows, lanes].astype(F32)

            for w, c, value in boxcars(load, channels):
                square = value * value
                sums[(k * WIDTHS + w) * channels + c] += square[:8] + square[8:]
        return 0

    lax.fori_loop(0, tall // 16 * lane_groups, add, 0)
    total = jnp.sum(jnp.sum(sums[...], axis=1), axis=1, keepdims=True)
    power[...] = jnp.broadcast_to(total, power.shape)


def smooth_power(me, odd, own, sides, down, across):
    _, channels, tall, broad = own.shape
    pairs = KERNELS * WIDTHS * channels
    halo = jax.ShapeDtypeStruct((KERNELS, 2 * EDGE, tall, broad), BF16)
    return pl.pallas_call(
        power_kernel,
        in_specs=[SMEM, SMEM] + [VMEM] * (3 + len(sides)),
        out_specs=[VMEM] * 2,
        out_shape=[halo, jax.ShapeDtypeStruct((pairs, LANES), F32)],
        scratch_shapes=[
            pltpu.VMEM((KERNELS, EDGE * tall, broad), BF16),
            pltpu.VMEM((pairs, 8, LANES), F32),
        ],
        compiler_params=params(24),
        cost_estimate=cost(2 * halo.size * (broad + 256), 8 * halo.size),
        name="smooth_power",
    )(me, odd, down, across, own, *sides)


def score_kernel(count, cells, own, halo, clips, *refs):
    layers, powers = (own, halo), refs[:count]
    out, factor = refs[-2:]
    channels, step_rows, broad = out.shape
    order = layer_order(channels)

    @pl.when(pl.program_id(0) == 0)
    def _():
        total = powers[0][...]
        for item in powers[1:]:
            total = total + item[...]
        noise = jnp.sqrt(total / cells + EPSILON)
        for k in range(KERNELS):
            for w in range(WIDTHS):
                rows = slice((k * WIDTHS + w) * channels, (k * WIDTHS + w + 1) * channels)
                scale = 10.0 / (clips[k, w].astype(F32) * noise[rows])
                factor[rows] = jnp.broadcast_to(scale[:, None], (channels,) + factor.shape[1:])

    lane_groups = broad // LANES
    base = pl.program_id(0) * step_rows

    def score(step, _):
        start = pl.multiple_of(step // lane_groups * 16, 16)
        rows = pl.ds(pl.multiple_of(base + start, 16), 16)
        lanes = pl.ds(pl.multiple_of(step % lane_groups * LANES, LANES), LANES)
        best = [None] * channels
        for k in range(KERNELS):

            def load(i, k=k):
                array, plane = order[i]
                return layers[array][k, plane, rows, lanes].astype(F32).reshape(2, 8, LANES)

            for w, c, value in boxcars(load, channels):
                value = jnp.abs(value) * factor[(k * WIDTHS + w) * channels + c]
                best[c] = value if best[c] is None else jnp.maximum(best[c], value)
        for c in range(channels):
            out[c, pl.ds(start, 16), lanes] = best[c].reshape(16, LANES)
        return 0

    lax.fori_loop(0, step_rows // 16 * lane_groups, score, 0)


def score(own, halo, clips, powers, cells):
    _, channels, tall, broad = own.shape
    pairs = KERNELS * WIDTHS * channels
    step = 32
    return pl.pallas_call(
        functools.partial(score_kernel, len(powers), cells),
        grid=(tall // step,),
        in_specs=[VMEM, VMEM, SMEM] + [VMEM] * len(powers),
        out_specs=pl.BlockSpec((channels, step, broad), lambda i: (0, i, 0)),
        out_shape=jax.ShapeDtypeStruct((channels, tall, broad), F32),
        scratch_shapes=[pltpu.VMEM((pairs, 8, LANES), F32)],
        compiler_params=params(14),
        cost_estimate=cost(40 * KERNELS * channels * tall * broad, 8 * own.size),
        name="score_cells",
    )(own, halo, clips, *powers)


def shards(across_table, down_table, pieces, beam, destination, clip_tenths):
    count = lax.axis_size("sky")
    links = lax.axis_size("freq")
    piece_count, channels = pieces.shape[:2]
    me = lax.axis_index("sky").astype(jnp.int32).reshape(1)
    across = jnp.asarray(across_table)
    down = jnp.asarray(down_table)

    strip = LANES // count
    parts = pieces.reshape(piece_count, channels, count, strip, LANES)
    beams = beam.reshape(piece_count, count, strip, LANES)
    packed = pack(me, destination, parts, beams, (1,))
    packed += pack(me, destination, parts, beams, tuple(range(2, count)))
    arrived = [exchange(block, "sky", k) for k, block in enumerate(packed, 1)]
    total, cover = gather_own(me, destination, parts, beams)
    strips = combine(me, total, cover, arrived, piece_count)
    tiles = [strips[0]] + [exchange(strips[k], "sky", k) for k in range(1, count)]
    odd = lax.rem(lax.axis_index("freq").astype(jnp.int32), 2).reshape(1)
    outer, inner = join(me, odd, tiles)
    outer_pairs = [(i, i + 1) for i in range(1, links - 1, 2)]
    inner_pairs = [(i, i + 1) for i in range(0, links - 1, 2)]
    sides = [
        lax.ppermute(block, "freq", pairs + [(target, source) for source, target in pairs])
        for block, pairs in ((outer, outer_pairs), (inner, inner_pairs))
    ]
    own = smooth(me, tiles, down, across)
    halo, power = smooth_power(me, odd, own, sides, down, across)
    powers = [power] + [exchange(power, "sky", k) for k in range(1, count)]
    cells = float(count * ROWB * LANES * COLB * LANES)
    return score(own, halo, clip_tenths, powers, cells)


def solution(mesh):
    count = mesh.shape["sky"]
    body = functools.partial(
        shards, across_matrices(COLB * LANES), down_matrices(count, ROWB * LANES // count)
    )
    return jax.shard_map(
        body,
        mesh=mesh,
        in_specs=(P("sky", "freq", None, None), P("sky", None, None), P("sky"), P()),
        out_specs=P("freq", "sky", None),
        check_vma=False,
    )
```
